128 devices in a mesh: blk: 8 (over y, x_lo), group: 16 (over z, x_hi, core).
Axes of the slice: x: 4 (x_hi: 2, x_lo: 2; x = x_hi * 2 + x_lo), y: 4, z: 4, core: 2. Of those that a mesh axis runs over, the one named last changes fastest.
Arguments:
- image_embeds: bfloat16 [16384, 768], P(('blk', 'group')), may hold values from -12 to 12
- text_embeds: bfloat16 [16384, 768], P(('blk', 'group')), may hold values from -12 to 12
- pair_weights: bfloat16 [16384], P(('blk', 'group')), may hold values from 0.19921875 to 5
- log_scale: float32 [1], replicated, may hold values from 2 to 2.5
- bias: float32 [1], replicated, may hold values from -15 to -11
Outputs:
- grad_image: float32 [16384, 768], P(('blk', 'group'))
- grad_text: float32 [16384, 768], P(('blk', 'group'))
- scalars: float32 [3], replicated
The draws below stay inside these ranges and needn't reach their ends.
All inputs are finite; a program needn't handle non-finite values.
Results may differ from the reference program's by a relative error of at most 0.0013.
The reference program's roundings to bfloat16 on the way count: a program that leaves them out, or rounds other values in their place, can miss the bound.
Values may be sent and summed in bfloat16 or wider, within the bound.
No kernel may reach another device: no remote copies, remote signals or barrier semaphores. Data moves between devices by JAX's collectives and lax.ppermute only.
A program may use at most 64 MiB of HBM per device.

```python
import math
import jax
import jax.numpy as jnp
from jax import lax

D = 768
TOKENS = 16384


def shared_parts(key):
    key_common, key_paired = jax.random.split(key)
    common = jax.random.normal(key_common, (D,), jnp.float32)
    paired = jax.random.normal(key_paired, (TOKENS, D), jnp.float32)
    return (common, paired)


def tower_rows(key, common, paired, noise_scale):
    key_amount, key_noise = jax.random.split(key)
    amount = jax.random.uniform(key_amount, (TOKENS, 1), jnp.float32, 0.4, 1.2)
    noises = noise_scale * jax.random.normal(key_noise, (TOKENS, D), jnp.float32)
    values = amount * common[None, :] + paired + noises
    return jnp.clip(values, -12.0, 12.0).astype(jnp.bfloat16)


def draw_image_embeds(key, part):
    common, paired = shared_parts(key)
    key = jax.random.fold_in(key, 11)
    return tower_rows(key, common, paired, 0.3)


def draw_text_embeds(key, part):
    common, paired = shared_parts(key)
    key = jax.random.fold_in(key, 23)
    return tower_rows(key, common, paired, 0.3)


def shard_levels(stream_key, shape, pieces, least, top_value):
    factor_of, own = 1.0, jax.random.fold_in(stream_key, 6)
    for position, parts in pieces:
        steps = jnp.exp(jax.random.uniform(jax.random.fold_in(own, position), (parts,), jnp.float32, least / len(pieces), top_value / len(pieces)))
        factor_of = factor_of * jnp.repeat(steps, shape[position] // parts).reshape([-1 if axis == position else 1 for axis in range(len(shape))])
    return factor_of


def setup_inputs(seed: int = 0) -> dict:
    arg_keys = jax.random.split(jax.random.key(seed), 6)
    image_embeds = draw_image_embeds(jax.random.fold_in(arg_keys[5], 71), 0)
    text_embeds = draw_text_embeds(jax.random.fold_in(arg_keys[5], 71), 0)
    pair_weights = jnp.clip(jnp.exp(math.log(5.0) - 3.2227897 * jax.random.uniform(arg_keys[2], (TOKENS,), jnp.float32) ** shard_levels(arg_keys[2], (TOKENS,), ((0, 128),), -0.2, 0.2)), 0.19921875, 5.0).astype(jnp.bfloat16)
    log_scale = jnp.clip(jax.random.uniform(arg_keys[3], (1,), jnp.float32, 2.0, 2.5), 2.0, 2.5)
    bias = jnp.clip(jax.random.uniform(arg_keys[4], (1,), jnp.float32, -15.0, -11.0), -15.0, -11.0)
    return {"image_embeds": image_embeds, "text_embeds": text_embeds, "pair_weights": pair_weights, "log_scale": log_scale, "bias": bias}


def normalize(values):
    wide = values.astype(jnp.float32)
    row_norm = jnp.sqrt(lax.optimization_barrier(jnp.sum(wide * wide, axis=1, keepdims=True)) + 1e-06)
    return (wide / row_norm, row_norm)

def normal_back(gradient, row_unit, row_norm):
    inner = lax.optimization_barrier(jnp.sum(row_unit * gradient, axis=1, keepdims=True))
    return (gradient - row_unit * inner) / row_norm

def reference(image_embeds, text_embeds, pair_weights, log_scale, bias):
    logit_scale = jnp.exp(log_scale[0])
    logit_bias = bias[0]
    img_unit, img_norm = normalize(image_embeds)
    txt_unit, txt_norm = normalize(text_embeds)
    img_bf = img_unit.astype(jnp.bfloat16)
    txt_bf = txt_unit.astype(jnp.bfloat16)
    weight_wide = pair_weights.astype(jnp.float32)
    weighted = (weight_wide[:, None] * img_bf.astype(jnp.float32)).astype(jnp.bfloat16)
    weight_total = jnp.sum(weight_wide)
    block_rows = 512 if TOKENS % 512 == 0 else TOKENS
    block_count = TOKENS // block_rows
    txt_ids = jnp.arange(TOKENS, dtype=jnp.int32)

    def advance(carried, block_index):
        text_acc, loss_sum, diff_sum, score_sum = carried
        row_start = (block_index * block_rows).astype(jnp.int32)
        img_rows = lax.dynamic_slice_in_dim(img_bf, row_start, block_rows, 0)
        row_weights = lax.dynamic_slice_in_dim(weight_wide, row_start, block_rows, 0)
        weighted_rows = lax.dynamic_slice_in_dim(weighted, row_start, block_rows, 0)
        scores = lax.dot_general(img_rows, txt_bf, (((1,), (1,)), ((), ())), preferred_element_type=jnp.float32)
        logits = logit_scale * scores + logit_bias
        img_ids = row_start + jnp.arange(block_rows, dtype=jnp.int32)
        matched = img_ids[:, None] == txt_ids[None, :]
        labels = jnp.where(matched, 1.0, 0.0).astype(jnp.float32)
        diffs = jax.nn.sigmoid(logits) - labels
        losses = jnp.where(matched, jax.nn.softplus(-logits), jax.nn.softplus(logits))
        coef_bf = diffs.astype(jnp.bfloat16)
        img_terms = jnp.dot(coef_bf, txt_bf, preferred_element_type=jnp.float32)
        text_acc = text_acc + lax.dot_general(coef_bf, weighted_rows, (((0,), (0,)), ((), ())), preferred_element_type=jnp.float32)
        loss_sum = loss_sum + jnp.sum(row_weights * lax.optimization_barrier(jnp.sum(losses, axis=1)))
        diff_sum = diff_sum + jnp.sum(row_weights * lax.optimization_barrier(jnp.sum(diffs, axis=1)))
        score_sum = score_sum + jnp.sum(row_weights * lax.optimization_barrier(jnp.sum(diffs * scores, axis=1)))
        return ((text_acc, loss_sum, diff_sum, score_sum), img_terms)
    zero = jnp.zeros((), jnp.float32)
    initial = (jnp.zeros((TOKENS, D), jnp.float32), zero, zero, zero)
    final, img_terms = lax.scan(advance, initial, jnp.arange(block_count, dtype=jnp.int32))
    text_acc, loss_sum, diff_sum, score_sum = final
    img_terms = img_terms.reshape(TOKENS, D)
    img_dir = logit_scale * weight_wide[:, None] * img_terms / weight_total
    txt_dir = logit_scale * text_acc / weight_total
    grad_image = float(TOKENS) * normal_back(img_dir, img_unit, img_norm)
    grad_text = float(TOKENS) * normal_back(txt_dir, txt_unit, txt_norm)
    scalars = jnp.stack([loss_sum / weight_total, logit_scale * score_sum / weight_total, diff_sum / weight_total])
    return (grad_image, grad_text, scalars)
```

```python
import functools

import jax
import jax.numpy as jnp
from jax import lax
from jax.experimental import pallas as pl
from jax.experimental.pallas import tpu as pltpu
from jax.sharding import PartitionSpec as P

F32 = jnp.float32
BF16 = jnp.bfloat16
SEND = jnp.float16
SIDE = 4
AXES = ("blk", "group")
LANES = 128
TAIL = 16
CONTRACT_LAST = (((1,), (1,)), ((), ()))
CONTRACT_FIRST = (((0,), (0,)), ((), ()))


def place(x, y, z, core):
    return (y * 2 + x % 2) * 16 + (z * 2 + x // 2) * 2 + core


def pairs(move):
    found = []
    for x in range(SIDE):
        for y in range(SIDE):
            for z in range(SIDE):
                for core in range(2):
                    found.append((place(x, y, z, core), place(*move(x, y, z, core))))
    return found


def send(values, move):
    return lax.ppermute(values, AXES, pairs(move))


def to_img_mate(x, y, z, c):
    return (x ^ 1, y, z, c)


def to_txt_mate(x, y, z, c):
    return (3 - x, y, z, c)


def to_sibling(x, y, z, c):
    return (x, y, z, 1 - c)


def along_y(step):
    return lambda x, y, z, c: (x, (y + step) % SIDE, z, c)


def along_z(step):
    return lambda x, y, z, c: (x, y, (z + step) % SIDE, c)


def row_norm_of(wide):
    return jnp.sqrt(jnp.sum(wide * wide, axis=1, keepdims=True) + 1e-06)


def column_of(weight_row, width):
    return jnp.transpose(jnp.broadcast_to(weight_row, (width, weight_row.shape[1])))


def prepare_kernel(img_ref, txt_ref, wgt_ref, img_out, txt_out):
    rows, width = img_ref.shape
    img = img_ref[...].astype(F32)
    img_out[pl.ds(0, rows), :] = (img / row_norm_of(img)).astype(BF16)
    img_out[pl.ds(rows, TAIL), :] = jnp.zeros((TAIL, width), BF16)
    img_out[pl.ds(rows, TAIL), pl.ds(0, rows)] = jnp.broadcast_to(wgt_ref[...], (TAIL, rows))
    txt = txt_ref[...].astype(F32)
    txt_out[...] = (txt / row_norm_of(txt)).astype(BF16)


def join_kernel(img_ref, img_mate, txt_ref, txt_mate, img_out, txt_out):
    rows, width = txt_ref.shape
    img_out[pl.ds(0, rows), :] = img_ref[pl.ds(0, rows), :]
    img_out[pl.ds(rows, rows), :] = img_mate[pl.ds(0, rows), :]
    img_out[pl.ds(2 * rows, TAIL), :] = img_ref[pl.ds(rows, TAIL), :]
    img_out[pl.ds(2 * rows, TAIL), pl.ds(rows, rows)] = img_mate[pl.ds(rows, TAIL), pl.ds(0, rows)]
    txt_out[pl.ds(0, rows), :] = txt_ref[...]
    txt_out[pl.ds(rows, rows), :] = txt_mate[...]


def pair_kernel(log_scale_ref, bias_ref, *refs):
    img_refs, txt_refs = refs[:8], refs[8:12]
    own_out, sib_out, txt_out, sums_out = refs[12:16]
    txt_all, weighted_all, coef_all = refs[16:]
    span, width = txt_refs[0].shape
    rows = span // 2
    scale = jnp.exp(jnp.full((1, LANES), log_scale_ref[0], F32))
    bias = bias_ref[0]
    for part in range(SIDE):
        txt_all[pl.ds(span * part, span), :] = txt_refs[part][...]
    zero = jnp.zeros((8, LANES), F32)
    loss, diff, score = zero, zero, zero
    same = lax.broadcasted_iota(jnp.int32, (rows, LANES), 0) == lax.broadcasted_iota(
        jnp.int32, (rows, LANES), 1
    )

    def fold(values):
        return jnp.sum(values.reshape(-1, 8, LANES), axis=0)

    for part in range(2 * SIDE):
        here = pl.ds(span * part, span)
        img = img_refs[part][pl.ds(0, span), :]
        weight = column_of(img_refs[part][pl.ds(span, TAIL), :][0:1, :span].astype(F32), LANES)
        weighted_all[here, :] = (img.astype(F32) * jnp.tile(weight, (1, width // LANES))).astype(
            BF16
        )
        scores = lax.dot_general(img, txt_all[...], CONTRACT_LAST, preferred_element_type=F32)
        for tile in range(SIDE * span // LANES):
            score_tile = scores[:, tile * LANES : (tile + 1) * LANES]
            grown = jnp.exp(score_tile * scale + bias)
            beyond = 1.0 + grown
            diffs = grown / beyond
            if part == 0 and tile == 0:
                diffs = jnp.concatenate(
                    [jnp.where(same, diffs[:rows] - 1.0, diffs[:rows]), diffs[rows:]], axis=0
                )
                matched = jnp.where(same, score_tile[:rows] * scale + bias, 0.0)
                loss = loss - fold(matched * weight[:rows])
            coef_all[here, pl.ds(tile * LANES, LANES)] = diffs.astype(BF16)
            if tile == 0:
                over, diff_row, score_row = grown, diffs, diffs * score_tile
            else:
                over = over * beyond + grown
                diff_row = diff_row + diffs
                score_row = score_row + diffs * score_tile
        loss = loss + fold(jnp.log1p(over) * weight)
        diff = diff + fold(diff_row * weight)
        score = score + fold(score_row * weight)
        out = own_out if part % 2 == 0 else sib_out
        out[part // 2] = jnp.dot(coef_all[here, :], txt_all[...], preferred_element_type=F32)
    sums_out[...] = jnp.zeros((8, LANES), F32)
    sums_out[0:1, :] = jnp.sum(loss, axis=0, keepdims=True)
    sums_out[1:2, :] = jnp.sum(score, axis=0, keepdims=True)
    sums_out[2:3, :] = jnp.sum(diff, axis=0, keepdims=True)
    sums_out[3:4, :] = img_refs[0][pl.ds(span, TAIL), :][0:1, :rows].astype(F32)
    for part in range(SIDE):
        txt_out[part] = lax.dot_general(
            coef_all[:, pl.ds(span * part, span)],
            weighted_all[...],
            CONTRACT_FIRST,
            preferred_element_type=F32,
        )


def finish_kernel(
    log_scale_ref, sums_ref, img_ref, txt_ref, wgt_ref, img_sum, txt_sum, img_out, txt_out, scalar_out
):
    rows, width = img_ref.shape
    scale = jnp.exp(jnp.full((1, LANES), log_scale_ref[0], F32))
    totals = jnp.sum(sums_ref[...], axis=1, keepdims=True)
    total = totals[3:4]
    pair_count = float(rows * 2 * SIDE**3)
    factor = jnp.tile(scale / total, (1, width // LANES))

    def back(gradient, values):
        norm = row_norm_of(values)
        unit = values / norm
        inner = jnp.sum(unit * gradient, axis=1, keepdims=True)
        return pair_count * (gradient - unit * inner) / norm

    weight = jnp.tile(column_of(wgt_ref[...].astype(F32), LANES), (1, width // LANES))
    img_out[...] = back(factor * weight * img_sum[...], img_ref[...].astype(F32))
    txt_out[...] = back(factor * txt_sum[...], txt_ref[...].astype(F32))
    ratio = jnp.broadcast_to(totals / total, (8, LANES))
    row = lax.broadcasted_iota(jnp.int32, (8, LANES), 0)
    scalar_out[...] = jnp.where(row == 1, scale * ratio, ratio)


IN_VMEM = pl.BlockSpec(memory_space=pltpu.VMEM)
IN_SMEM = pl.BlockSpec(memory_space=pltpu.SMEM)


def call(kernel, shapes, scalars, arrays, flops, moved, scratch=(), limit=16):
    return pl.pallas_call(
        kernel,
        out_shape=[jax.ShapeDtypeStruct(shape, kind) for shape, kind in shapes],
        in_specs=[IN_SMEM] * len(scalars) + [IN_VMEM] * len(arrays),
        out_specs=[IN_VMEM] * len(shapes),
        scratch_shapes=[pltpu.VMEM(shape, kind) for shape, kind in scratch],
        compiler_params=pltpu.CompilerParams(vmem_limit_bytes=limit * 2**20),
        cost_estimate=pl.CostEstimate(flops=flops, bytes_accessed=moved, transcendentals=0),
    )(*scalars, *arrays)


def body(image_embeds, text_embeds, pair_weights, log_scale, bias):
    rows, width = image_embeds.shape
    span = 2 * rows
    weight_row = pair_weights.reshape(1, rows)
    img_own, txt_own = call(
        prepare_kernel,
        [((rows + TAIL, width), BF16), ((rows, width), BF16)],
        [],
        [image_embeds, text_embeds, weight_row],
        2 * 8 * rows * width,
        8 * rows * width,
    )
    img_pair, txt_pair = call(
        join_kernel,
        [((span + TAIL, width), BF16), ((span, width), BF16)],
        [],
        [img_own, send(img_own, to_img_mate), txt_own, send(txt_own, to_txt_mate)],
        1,
        16 * rows * width,
    )
    steps = (1, 3, 2)
    img_near = {0: img_pair}
    txt_near = {0: txt_pair}
    for step in steps:
        img_near[step] = send(img_pair, along_z(step))
        txt_near[step] = send(txt_pair, along_y(step))
    images = []
    for step in (0,) + steps:
        images += [img_near[step], send(img_near[step], to_sibling)]
    texts = [txt_near[step] for step in (0,) + steps]
    tall = 2 * SIDE * span
    own_part, sib_part, txt_part, sums = call(
        pair_kernel,
        [((SIDE, span, width), F32)] * 3 + [((8, LANES), F32)],
        [log_scale, bias],
        images + texts,
        6 * tall * SIDE * span * width,
        20 * tall * width,
        [((SIDE * span, width), BF16), ((tall, width), BF16), ((tall, SIDE * span), BF16)],
        40,
    )
    txt_sum = txt_part[0]
    for place_, step in enumerate(steps):
        moved = send(txt_part[place_ + 1].astype(SEND), along_y(-step))
        txt_sum = txt_sum + moved.astype(F32)
    img_sum = own_part[0] + send(sib_part[0], to_sibling)
    for place_, step in enumerate(steps):
        joint = own_part[place_ + 1] + send(sib_part[place_ + 1], to_sibling)
        img_sum = img_sum + send(joint.astype(SEND), along_z(-step)).astype(F32)
    txt_sum = txt_sum[:rows] + send(txt_sum[rows:].astype(SEND), to_txt_mate).astype(F32)
    img_sum = img_sum[:rows] + send(img_sum[rows:].astype(SEND), to_img_mate).astype(F32)
    for move in (
        to_sibling,
        to_img_mate,
        to_txt_mate,
        lambda x, y, z, c: (x, y ^ 1, z, c),
        lambda x, y, z, c: (x, 3 - y, z, c),
        lambda x, y, z, c: (x, y, z ^ 1, c),
        lambda x, y, z, c: (x, y, 3 - z, c),
    ):
        sums = sums + send(sums, move)
    grad_image, grad_text, scalars = call(
        finish_kernel,
        [((rows, width), F32), ((rows, width), F32), ((8, LANES), F32)],
        [log_scale],
        [sums, image_embeds, text_embeds, weight_row, img_sum, txt_sum],
        2 * 12 * rows * width,
        24 * rows * width,
    )
    return grad_image, grad_text, scalars[:3, 0]


def solution(mesh):
    placed = (P(AXES, None), P(AXES, None), P(AXES), P(), P())
    return jax.shard_map(
        body,
        mesh=mesh,
        in_specs=placed,
        out_specs=(P(AXES, None), P(AXES, None), P()),
        check_vma=False,
    )
```

```python
import functools

import jax
import jax.numpy as jnp
from jax import lax
from jax.experimental import pallas as pl
from jax.experimental.pallas import tpu as pltpu
from jax.sharding import PartitionSpec as P

F32 = jnp.float32
BF16 = jnp.bfloat16
SEND = jnp.float16
SIDE = 4
AXES = ("blk", "group")
LANES = 128
TAIL = 16
CONTRACT_LAST = (((1,), (1,)), ((), ()))
CONTRACT_FIRST = (((0,), (0,)), ((), ()))


def place(x, y, z, core):
    return (y * 2 + x % 2) * 16 + (z * 2 + x // 2) * 2 + core


def pairs(move):
    found = []
    for x in range(SIDE):
        for y in range(SIDE):
            for z in range(SIDE):
                for core in range(2):
                    found.append((place(x, y, z, core), place(*move(x, y, z, core))))
    return found


def send(values, move):
    return lax.ppermute(values, AXES, pairs(move))


def pair_move(x, y, z, core):
    return (x ^ 1 if core == 0 else 3 - x, y, z, core)


def column_move(x, y, z, core):
    return (3 - x if core == 0 else x ^ 1, y, z, core)


def to_sibling(x, y, z, core):
    return (x, y, z, 1 - core)


def pair_step(step):
    return lambda x, y, z, core: (
        (x, y, (z + step) % SIDE, core) if core == 0 else (x, (y + step) % SIDE, z, core)
    )


def column_step(step):
    return lambda x, y, z, core: (
        (x, (y + step) % SIDE, z, core) if core == 0 else (x, y, (z + step) % SIDE, core)
    )


STEPS = (1, 3, 2)


def on_core():
    return lax.rem(lax.axis_index("group"), 2)


def row_norm_of(wide):
    return jnp.sqrt(jnp.sum(wide * wide, axis=1, keepdims=True) + 1e-06)


def column_of(weight_row, width):
    return jnp.transpose(jnp.broadcast_to(weight_row, (width, weight_row.shape[1])))


def prepare_kernel(img_ref, txt_ref, wgt_ref, pair_out, column_out):
    rows, width = img_ref.shape
    img = img_ref[...].astype(F32)
    img = (img / row_norm_of(img)).astype(BF16)
    txt = txt_ref[...].astype(F32)
    txt = (txt / row_norm_of(txt)).astype(BF16)
    here = pl.ds(0, rows)
    for out in (pair_out, column_out):
        out[pl.ds(rows, TAIL), :] = jnp.zeros((TAIL, width), BF16)
        out[pl.ds(rows, TAIL), pl.ds(0, rows)] = jnp.broadcast_to(wgt_ref[...], (TAIL, rows))

    @pl.when(on_core() == 0)
    def _():
        pair_out[here, :] = img
        column_out[here, :] = txt

    @pl.when(on_core() == 1)
    def _():
        pair_out[here, :] = txt
        column_out[here, :] = img


def join_kernel(*refs):
    pair_refs, column_refs, (pair_out, column_out) = refs[:2], refs[2:6], refs[6:]
    for blocks, out in ((pair_refs, pair_out), (column_refs, column_out)):
        rows = blocks[0].shape[0] - TAIL
        tail = pl.ds(len(blocks) * rows, TAIL)
        out[tail, :] = jnp.zeros((TAIL, out.shape[1]), BF16)
        for index, block in enumerate(blocks):
            out[pl.ds(index * rows, rows), :] = block[pl.ds(0, rows), :]
            out[tail, pl.ds(index * rows, rows)] = block[pl.ds(rows, TAIL), pl.ds(0, rows)]


def take_pairs(blocks, rows_out, wgt_out):
    span = blocks[0].shape[0] - TAIL
    for index, block in enumerate(blocks):
        rows_out[pl.ds(index * span, span), :] = block[pl.ds(0, span), :]
        if wgt_out is not None:
            weight = block[pl.ds(span, TAIL), :][0:1, :span].astype(F32)
            wgt_out[pl.ds(index * span, span), :] = column_of(weight, LANES)


def take_columns(blocks, rows_out, wgt_out):
    span = blocks[0].shape[0] - TAIL
    rows = span // SIDE
    for chip, block in enumerate(blocks):
        for index in range(SIDE):
            there = pl.ds((2 * index + chip) * rows, rows)
            rows_out[there, :] = block[pl.ds(index * rows, rows), :]
            if wgt_out is not None:
                weight = block[pl.ds(span, TAIL), :][0:1, index * rows : (index + 1) * rows]
                wgt_out[there, :] = column_of(weight.astype(F32), LANES)


def score_part(img_all, wgt_all, txt_all, scale, bias, own, coef_out, weighted_out, grad_out, sums_out):
    count, width = img_all.shape
    span = 256
    rows = 128
    zero = jnp.zeros((8, LANES), F32)
    loss, diff, score = zero, zero, zero
    same = lax.broadcasted_iota(jnp.int32, (rows, LANES), 0) == lax.broadcasted_iota(
        jnp.int32, (rows, LANES), 1
    )

    def fold(values):
        return jnp.sum(values.reshape(-1, 8, LANES), axis=0)

    for part in range(count // span):
        here = pl.ds(span * part, span)
        img = img_all[here, :]
        weight = wgt_all[here, :]
        weighted_out[here, :] = (img.astype(F32) * jnp.tile(weight, (1, width // LANES))).astype(
            BF16
        )
        scores = lax.dot_general(img, txt_all[...], CONTRACT_LAST, preferred_element_type=F32)
        for tile in range(scores.shape[1] // LANES):
            score_tile = scores[:, tile * LANES : (tile + 1) * LANES]
            grown = jnp.exp(score_tile * scale + bias)
            beyond = 1.0 + grown
            diffs = grown / beyond
            if own and part == 0 and tile == 0:
                diffs = jnp.concatenate(
                    [jnp.where(same, diffs[:rows] - 1.0, diffs[:rows]), diffs[rows:]], axis=0
                )
                matched = jnp.where(same, score_tile[:rows] * scale + bias, 0.0)
                loss = loss - fold(matched * weight[:rows])
            coef_out[here, pl.ds(tile * LANES, LANES)] = diffs.astype(BF16)
            if tile == 0:
                over, diff_row, score_row = grown, diffs, diffs * score_tile
            else:
                over = over * beyond + grown
                diff_row = diff_row + diffs
                score_row = score_row + diffs * score_tile
        loss = loss + fold(jnp.log1p(over) * weight)
        diff = diff + fold(diff_row * weight)
        score = score + fold(score_row * weight)
        grad_out[here, :] = jnp.dot(coef_out[here, :], txt_all[...], preferred_element_type=F32)
    sums_out[0] = loss
    sums_out[1] = score
    sums_out[2] = diff


def sibling_kernel(log_scale_ref, bias_ref, *refs):
    pair_refs, column_refs, pair_sib, column_sib = refs[:4], refs[4:6], refs[6:10], refs[10:12]
    grad_out, coef_out, weighted_out, txt_all, sums_out, img_all, wgt_all = refs[12:]

    @pl.when(on_core() == 0)
    def _():
        take_columns(column_refs, txt_all, None)
        take_columns(column_sib, img_all, wgt_all)

    @pl.when(on_core() == 1)
    def _():
        take_pairs(pair_refs, txt_all, None)
        take_pairs(pair_sib, img_all, wgt_all)

    scale = jnp.exp(jnp.full((1, LANES), log_scale_ref[0], F32))
    score_part(
        img_all, wgt_all, txt_all, scale, bias_ref[0], False, coef_out, weighted_out, grad_out, sums_out
    )


def own_kernel(log_scale_ref, bias_ref, *refs):
    pair_refs, column_refs, txt_all = refs[:4], refs[4:6], refs[6]
    grad_out, coef_out, weighted_out, sums_out, img_all, wgt_all = refs[7:]

    @pl.when(on_core() == 0)
    def _():
        take_pairs(pair_refs, img_all, wgt_all)

    @pl.when(on_core() == 1)
    def _():
        take_columns(column_refs, img_all, wgt_all)

    scale = jnp.exp(jnp.full((1, LANES), log_scale_ref[0], F32))
    score_part(
        img_all, wgt_all, txt_all, scale, bias_ref[0], True, coef_out, weighted_out, grad_out, sums_out
    )


def text_kernel(
    sib_sums,
    own_sums,
    wgt_ref,
    sib_coef,
    own_coef,
    sib_weighted,
    own_weighted,
    own_grad,
    moved_grad,
    pair_keep,
    pair_send,
    column_keep,
    column_send,
    sums_out,
):
    rows = wgt_ref.shape[1]
    span = 2 * rows

    def put_pair(index, values):
        if index == 0:
            pair_keep[...] = values
        else:
            pair_send[index - 1] = values

    def put_column(index, values):
        there = pl.ds(index * rows, rows)
        column_keep[there, :] = values[:rows]
        column_send[there, :] = values[rows:]

    for index in range(SIDE):
        here = pl.ds(span * index, span)
        img = own_grad[here, :] + moved_grad[here, :]
        txt = lax.dot_general(
            own_coef[:, here], own_weighted[...], CONTRACT_FIRST, preferred_element_type=F32
        ) + lax.dot_general(
            sib_coef[:, here], sib_weighted[...], CONTRACT_FIRST, preferred_element_type=F32
        )
        first = on_core() == 0
        put_pair(index, jnp.where(first, img, txt))
        put_column(index, jnp.where(first, txt, img))
    lane = lax.broadcasted_iota(jnp.int32, (1, LANES), 1)
    row = jnp.where(lane == 3, jnp.sum(wgt_ref[...].astype(F32), axis=1, keepdims=True), 0.0)
    for kind in range(3):
        part = jnp.sum(sib_sums[kind] + own_sums[kind], axis=0, keepdims=True)
        row = row + jnp.where(lane == kind, jnp.sum(part, axis=1, keepdims=True), 0.0)
    sums_out[...] = jnp.broadcast_to(row, sums_out.shape)


def finish_kernel(
    log_scale_ref, sums_ref, img_ref, txt_ref, wgt_ref, pair_sum, column_sum, img_out, txt_out, scalar_out
):
    rows, width = img_ref.shape
    scale = jnp.exp(jnp.full((1, LANES), log_scale_ref[0], F32))
    lane = lax.broadcasted_iota(jnp.int32, (1, LANES), 1)
    sums = jnp.sum(sums_ref[...], axis=0, keepdims=True)
    total = jnp.sum(jnp.where(lane == 3, sums, 0.0), axis=1, keepdims=True)
    pair_count = float(rows * 2 * SIDE**3)
    factor = jnp.tile(scale / total, (1, width // LANES))
    first = on_core() == 0

    def back(gradient, values):
        norm = row_norm_of(values)
        unit = values / norm
        inner = jnp.sum(unit * gradient, axis=1, keepdims=True)
        return pair_count * (gradient - unit * inner) / norm

    weight = jnp.tile(column_of(wgt_ref[...].astype(F32), LANES), (1, width // LANES))
    img_sum = jnp.where(first, pair_sum[...], column_sum[...])
    txt_sum = jnp.where(first, column_sum[...], pair_sum[...])
    img_out[...] = back(factor * weight * img_sum, img_ref[...].astype(F32))
    txt_out[...] = back(factor * txt_sum, txt_ref[...].astype(F32))
    ratio = sums / total
    scalar_out[...] = jnp.broadcast_to(jnp.where(lane == 1, scale * ratio, ratio), scalar_out.shape)


VMEM_MIB = 24
IN_VMEM = pl.BlockSpec(memory_space=pltpu.VMEM)
IN_SMEM = pl.BlockSpec(memory_space=pltpu.SMEM)


def call(kernel, shapes, scalars, arrays, flops, moved, scratch=(), limit=16):
    return pl.pallas_call(
        kernel,
        out_shape=[jax.ShapeDtypeStruct(shape, kind) for shape, kind in shapes],
        in_specs=[IN_SMEM] * len(scalars) + [IN_VMEM] * len(arrays),
        out_specs=[IN_VMEM] * len(shapes),
        scratch_shapes=[pltpu.VMEM(shape, kind) for shape, kind in scratch],
        compiler_params=pltpu.CompilerParams(vmem_limit_bytes=limit * 2**20),
        cost_estimate=pl.CostEstimate(flops=flops, bytes_accessed=moved, transcendentals=0),
    )(*scalars, *arrays)


def body(image_embeds, text_embeds, pair_weights, log_scale, bias):
    rows, width = image_embeds.shape
    span, tall = 2 * rows, 2 * SIDE * rows
    devices = 2 * SIDE**3
    weight_row = pair_weights.reshape(1, rows)
    pair_own, column_own = call(
        prepare_kernel,
        [((rows + TAIL, width), BF16)] * 2,
        [],
        [image_embeds, text_embeds, weight_row],
        2 * 8 * rows * width,
        8 * rows * width,
    )
    column_near = [column_own] + [send(column_own, column_step(step)) for step in STEPS]
    pair_near = [pair_own, send(pair_own, pair_move)]
    pair_all, column_all = call(
        join_kernel,
        [((span + TAIL, width), BF16), ((SIDE * rows + TAIL, width), BF16)],
        [],
        pair_near + column_near,
        1,
        24 * rows * width,
    )
    pairs_in = [pair_all] + [send(pair_all, pair_step(step)) for step in STEPS]
    columns_in = [column_all, send(column_all, column_move)]
    pairs_sib = [send(block, to_sibling) for block in pairs_in]
    columns_sib = [send(block, to_sibling) for block in columns_in]
    half = 4 * tall * tall * width
    square = (tall, tall)
    flat = (tall, width)
    keep = [((tall, width), BF16), ((tall, LANES), F32)]
    sums_shape = ((3, 8, LANES), F32)
    sib_grad, sib_coef, sib_weighted, txt_all, sib_sums = call(
        sibling_kernel,
        [(flat, F32), (square, BF16), (flat, BF16), (flat, BF16), sums_shape],
        [log_scale, bias],
        pairs_in + columns_in + pairs_sib + columns_sib,
        half,
        16 * tall * width,
        keep,
        VMEM_MIB,
    )
    moved_grad = send(sib_grad, to_sibling)
    own_grad, own_coef, own_weighted, own_sums = call(
        own_kernel,
        [(flat, F32), (square, BF16), (flat, BF16), sums_shape],
        [log_scale, bias],
        pairs_in + columns_in + [txt_all],
        half,
        16 * tall * width,
        keep,
        VMEM_MIB,
    )
    pair_keep, pair_send, column_keep, column_send, sums = call(
        text_kernel,
        [
            ((span, width), F32),
            ((SIDE - 1, span, width), F32),
            ((SIDE * rows, width), F32),
            ((SIDE * rows, width), F32),
            ((devices, LANES), F32),
        ],
        [],
        [sib_sums, own_sums, weight_row, sib_coef, own_coef, sib_weighted, own_weighted]
        + [own_grad, moved_grad],
        half,
        24 * tall * width,
        (),
        VMEM_MIB,
    )
    column_sum = column_keep + send(column_send.astype(SEND), column_move).astype(F32)
    pair_sum = pair_keep
    for index, step in enumerate(STEPS):
        pair_sum = pair_sum + send(pair_send[index].astype(SEND), pair_step(-step)).astype(F32)
    all_sums = lax.all_to_all(sums, AXES, 0, 0, tiled=True)
    pair_last = pair_sum[:rows] + send(pair_sum[rows:].astype(SEND), pair_move).astype(F32)
    column_last = column_sum[:rows]
    for index, step in enumerate(STEPS):
        block = column_sum[(index + 1) * rows : (index + 2) * rows]
        column_last = column_last + send(block.astype(SEND), column_step(-step)).astype(F32)
    grad_image, grad_text, scalars = call(
        finish_kernel,
        [((rows, width), F32), ((rows, width), F32), ((8, LANES), F32)],
        [log_scale],
        [all_sums, image_embeds, text_embeds, weight_row, pair_last, column_last],
        2 * 12 * rows * width,
        24 * rows * width,
    )
    return grad_image, grad_text, scalars[0, :3]


def solution(mesh):
    placed = (P(AXES, None), P(AXES, None), P(AXES), P(), P())
    return jax.shard_map(
        body,
        mesh=mesh,
        in_specs=placed,
        out_specs=(P(AXES, None), P(AXES, None), P()),
        check_vma=False,
    )
```

```python
import functools

import jax
import jax.numpy as jnp
from jax import lax
from jax.experimental import pallas as pl
from jax.experimental.pallas import tpu as pltpu
from jax.sharding import PartitionSpec as P

F32 = jnp.float32
BF16 = jnp.bfloat16
SEND = jnp.float16
SIDE = 4
AXES = ("blk", "group")
LANES = 128
LOG2_E = 1.4426950408889634
TAIL = 16
CONTRACT_LAST = (((1,), (1,)), ((), ()))
CONTRACT_FIRST = (((0,), (0,)), ((), ()))


def place(x, y, z, core):
    return (y * 2 + x % 2) * 16 + (z * 2 + x // 2) * 2 + core


def pairs(move):
    found = []
    for x in range(SIDE):
        for y in range(SIDE):
            for z in range(SIDE):
                for core in range(2):
                    found.append((place(x, y, z, core), place(*move(x, y, z, core))))
    return found


def send(values, move):
    return lax.ppermute(values, AXES, pairs(move))


def pair_move(x, y, z, core):
    return (x ^ 1 if core == 0 else 3 - x, y, z, core)


def column_move(x, y, z, core):
    return (3 - x if core == 0 else x ^ 1, y, z, core)


def to_sibling(x, y, z, core):
    return (x, y, z, 1 - core)


def pair_step(step):
    return lambda x, y, z, core: (
        (x, y, (z + step) % SIDE, core) if core == 0 else (x, (y + step) % SIDE, z, core)
    )


def column_step(step):
    return lambda x, y, z, core: (
        (x, (y + step) % SIDE, z, core) if core == 0 else (x, y, (z + step) % SIDE, core)
    )


STEPS = (1, 3, 2)


def on_core():
    return lax.rem(lax.axis_index("group"), 2)


def row_norm_of(wide):
    return jnp.sqrt(jnp.sum(wide * wide, axis=1, keepdims=True) + 1e-06)


def column_of(weight_row, width):
    return jnp.transpose(jnp.broadcast_to(weight_row, (width, weight_row.shape[1])))


def prepare_kernel(img_ref, txt_ref, wgt_ref, pair_out, column_out):
    rows, width = img_ref.shape
    img = img_ref[...].astype(F32)
    img = (img / row_norm_of(img)).astype(BF16)
    txt = txt_ref[...].astype(F32)
    txt = (txt / row_norm_of(txt)).astype(BF16)
    here = pl.ds(0, rows)
    for out in (pair_out, column_out):
        out[pl.ds(rows, TAIL), :] = jnp.zeros((TAIL, width), BF16)
        out[pl.ds(rows, TAIL), pl.ds(0, rows)] = jnp.broadcast_to(wgt_ref[...], (TAIL, rows))

    @pl.when(on_core() == 0)
    def _():
        pair_out[here, :] = img
        column_out[here, :] = txt

    @pl.when(on_core() == 1)
    def _():
        pair_out[here, :] = txt
        column_out[here, :] = img


def join_kernel(log_scale_ref, bias_ref, *refs):
    pair_refs, column_refs, (pair_out, column_out, given) = refs[:2], refs[2:6], refs[6:]
    given[0:1, :] = jnp.exp(jnp.full((1, LANES), log_scale_ref[0], F32))
    given[1:2, :] = jnp.full((1, LANES), bias_ref[0], F32)
    for blocks, out in ((pair_refs, pair_out), (column_refs, column_out)):
        rows = blocks[0].shape[0] - TAIL
        tail = pl.ds(len(blocks) * rows, TAIL)
        out[tail, :] = jnp.zeros((TAIL, out.shape[1]), BF16)
        for index, block in enumerate(blocks):
            out[pl.ds(index * rows, rows), :] = block[pl.ds(0, rows), :]
            out[tail, pl.ds(index * rows, rows)] = block[pl.ds(rows, TAIL), pl.ds(0, rows)]


def weights_of(block, rows, first):
    return block[pl.ds(2 * rows, TAIL), :][0:1, first : first + rows].astype(F32)


def take_pairs(blocks, rows_out, wgt_out):
    rows = rows_out.shape[0] // (2 * SIDE)
    for step, block in enumerate(blocks):
        for chip in range(2):
            there = pl.ds((chip * SIDE + step) * rows, rows)
            rows_out[there, :] = block[pl.ds(chip * rows, rows), :]
            if wgt_out is not None:
                wgt_out[there, :] = column_of(weights_of(block, rows, chip * rows), LANES)


def take_columns(blocks, rows_out, wgt_out):
    span = rows_out.shape[0] // len(blocks)
    for index, block in enumerate(blocks):
        there = pl.ds(index * span, span)
        rows_out[there, :] = block[pl.ds(0, span), :]
        if wgt_out is not None:
            weight = block[pl.ds(span, TAIL), :][0:1, :span].astype(F32)
            wgt_out[there, :] = column_of(weight, LANES)


def score_part(img_all, wgt_all, txt_all, scale, bias, first, coef_out, weighted_out, grad_out, sums_out):
    count, width = img_all.shape
    scale_two, bias_two = scale * LOG2_E, bias * LOG2_E
    span = 256
    rows = 128
    zero = jnp.zeros((8, LANES), F32)
    loss, diff, score = zero, zero, zero
    same = lax.broadcasted_iota(jnp.int32, (rows, LANES), 0) == lax.broadcasted_iota(
        jnp.int32, (rows, LANES), 1
    )

    def fold(values):
        return jnp.sum(values.reshape(-1, 8, LANES), axis=0)

    def scores_of(part):
        img = img_all[pl.ds(span * part, span), :]
        return lax.dot_general(img, txt_all[...], CONTRACT_LAST, preferred_element_type=F32)

    def gradient_of(part):
        here = pl.ds(span * part, span)
        there = pl.ds(first + span * part, span)
        grad_out[here, :] = jnp.dot(coef_out[there, :], txt_all[...], preferred_element_type=F32)

    parts = count // span
    scores = scores_of(0)
    for part in range(parts):
        next_scores = scores_of(part + 1) if part + 1 < parts else None
        if part:
            gradient_of(part - 1)
        here = pl.ds(span * part, span)
        there = pl.ds(first + span * part, span)
        weight = wgt_all[here, :]
        weighted_out[there, :] = (
            img_all[here, :].astype(F32) * jnp.tile(weight, (1, width // LANES))
        ).astype(BF16)
        for tile in range(scores.shape[1] // LANES):
            score_tile = scores[:, tile * LANES : (tile + 1) * LANES]
            grown = jnp.exp2(score_tile * scale_two + bias_two)
            beyond = 1.0 + grown
            diffs = grown / beyond
            if first == 0 and part == 0 and tile == 0:
                diffs = jnp.concatenate(
                    [jnp.where(same, diffs[:rows] - 1.0, diffs[:rows]), diffs[rows:]], axis=0
                )
                matched = jnp.where(same, score_tile[:rows] * scale + bias, 0.0)
                loss = loss - fold(matched * weight[:rows])
            coef_out[there, pl.ds(tile * LANES, LANES)] = diffs.astype(BF16)
            if tile == 0:
                over, diff_row, score_row = grown, diffs, diffs * score_tile
            else:
                over = over * beyond + grown
                diff_row = diff_row + diffs
                score_row = score_row + diffs * score_tile
        loss = loss + fold(jnp.log1p(over) * weight)
        diff = diff + fold(diff_row * weight)
        score = score + fold(score_row * weight)
        scores = next_scores
    gradient_of(parts - 1)
    sums_out[0] = loss
    sums_out[1] = score
    sums_out[2] = diff


def own_kernel(given, *refs):
    pair_refs, column_refs = refs[:4], refs[4:6]
    grad_out, coef_out, weighted_out, sums_out, txt_all, img_all, wgt_all = refs[6:]

    @pl.when(on_core() == 0)
    def _():
        take_pairs(pair_refs, img_all, wgt_all)
        take_columns(column_refs, txt_all, None)

    @pl.when(on_core() == 1)
    def _():
        take_columns(column_refs, img_all, wgt_all)
        take_pairs(pair_refs, txt_all, None)

    score_part(
        img_all, wgt_all, txt_all, given[0:1, :], given[1:2, :], 0, coef_out, weighted_out, grad_out, sums_out
    )


def sibling_kernel(chip, given, *refs):
    pair_refs, column_ref, txt_all = refs[:4], refs[4], refs[5]
    grad_out, coef_out, weighted_out, sums_out, img_all, wgt_all = refs[8:]
    span = img_all.shape[0]
    rows = span // SIDE

    @pl.when(on_core() == 0)
    def _():
        take_columns((column_ref,), img_all, wgt_all)

    @pl.when(on_core() == 1)
    def _():
        for step, block in enumerate(pair_refs):
            there = pl.ds(step * rows, rows)
            img_all[there, :] = block[pl.ds(chip * rows, rows), :]
            wgt_all[there, :] = column_of(weights_of(block, rows, chip * rows), LANES)

    score_part(
        img_all, wgt_all, txt_all, given[0:1, :], given[1:2, :], (2 + chip) * span, coef_out, weighted_out, grad_out, sums_out
    )


def text_kernel(*refs):
    sums_refs, wgt_ref, coef, weighted = refs[:3], *refs[3:6]
    near_out, far_out, sums_out = refs[6:]
    span = near_out.shape[0]
    for chip, out in enumerate((near_out, far_out)):
        here = pl.ds(chip * span, span)
        out[...] = lax.dot_general(
            coef[:, here], weighted[...], CONTRACT_FIRST, preferred_element_type=F32
        )
    lane = lax.broadcasted_iota(jnp.int32, (1, LANES), 1)
    row = jnp.where(lane == 3, jnp.sum(wgt_ref[...].astype(F32), axis=1, keepdims=True), 0.0)
    for kind in range(3):
        part = jnp.sum(sum(ref[kind] for ref in sums_refs), axis=0, keepdims=True)
        row = row + jnp.where(lane == kind, jnp.sum(part, axis=1, keepdims=True), 0.0)
    sums_out[...] = jnp.broadcast_to(row, sums_out.shape)


def merge_kernel(own_grad, near_moved, far_moved, near_txt, far_txt, *outs):
    pair_keep, pair_send, column_keep, column_send = outs
    span = near_txt.shape[0]
    rows = span // SIDE

    def put_pair(chip, step, values):
        there = pl.ds(chip * rows, rows)
        if step == 0:
            pair_keep[there, :] = values
        else:
            pair_send[step - 1, there, :] = values

    for chip, (moved, txt, column) in enumerate(
        ((near_moved, near_txt, column_keep), (far_moved, far_txt, column_send))
    ):
        for step in range(SIDE):
            here = pl.ds(step * rows, rows)
            img_here = pl.ds(chip * span + step * rows, rows)

            @pl.when(on_core() == 0)
            def _():
                put_pair(chip, step, own_grad[img_here, :] + moved[here, :])
                column[here, :] = txt[here, :]

            @pl.when(on_core() == 1)
            def _():
                put_pair(chip, step, txt[here, :])
                column[here, :] = own_grad[img_here, :] + moved[here, :]


def finish_kernel(
    given, sums_ref, img_ref, txt_ref, wgt_ref, pair_sum, column_sum, img_out, txt_out, scalar_out
):
    rows, width = img_ref.shape
    scale = given[0:1, :]
    lane = lax.broadcasted_iota(jnp.int32, (1, LANES), 1)
    sums = jnp.sum(sums_ref[...], axis=0, keepdims=True)
    total = jnp.sum(jnp.where(lane == 3, sums, 0.0), axis=1, keepdims=True)
    pair_count = float(rows * 2 * SIDE**3)
    factor = jnp.tile(scale / total, (1, width // LANES))
    first = on_core() == 0

    def back(gradient, values):
        norm = row_norm_of(values)
        unit = values / norm
        inner = jnp.sum(unit * gradient, axis=1, keepdims=True)
        return pair_count * (gradient - unit * inner) / norm

    weight = jnp.tile(column_of(wgt_ref[...].astype(F32), LANES), (1, width // LANES))
    img_sum = jnp.where(first, pair_sum[...], column_sum[...])
    txt_sum = jnp.where(first, column_sum[...], pair_sum[...])
    img_out[...] = back(factor * weight * img_sum, img_ref[...].astype(F32))
    txt_out[...] = back(factor * txt_sum, txt_ref[...].astype(F32))
    ratio = jnp.where(lane == 1, scale, 1.0) * sums / total
    for kind in range(3):
        scalar_out[kind] = jnp.sum(jnp.where(lane == kind, ratio, 0.0))


VMEM_MIB = 24
IN_VMEM = pl.BlockSpec(memory_space=pltpu.VMEM)
IN_SMEM = pl.BlockSpec(memory_space=pltpu.SMEM)


def call(kernel, shapes, scalars, arrays, flops, moved, scratch=(), limit=16, aliases=None):
    return pl.pallas_call(
        kernel,
        out_shape=[jax.ShapeDtypeStruct(shape, kind) for shape, kind in shapes],
        in_specs=[IN_SMEM] * len(scalars) + [IN_VMEM] * len(arrays),
        out_specs=[IN_SMEM if len(shape) == 1 else IN_VMEM for shape, kind in shapes],
        scratch_shapes=list(scratch),
        input_output_aliases=aliases or {},
        compiler_params=pltpu.CompilerParams(vmem_limit_bytes=limit * 2**20),
        cost_estimate=pl.CostEstimate(flops=flops, bytes_accessed=moved, transcendentals=0),
    )(*scalars, *arrays)


def body(image_embeds, text_embeds, pair_weights, log_scale, bias):
    rows, width = image_embeds.shape
    span, tall = 2 * rows, 2 * SIDE * rows
    devices = 2 * SIDE**3
    weight_row = pair_weights.reshape(1, rows)
    pair_own, column_own = call(
        prepare_kernel,
        [((rows + TAIL, width), BF16)] * 2,
        [],
        [image_embeds, text_embeds, weight_row],
        2 * 8 * rows * width,
        8 * rows * width,
    )
    column_near = [column_own] + [send(column_own, column_step(step)) for step in STEPS]
    pair_near = [pair_own, send(pair_own, pair_move)]
    pair_all, column_all, given = call(
        join_kernel,
        [((span + TAIL, width), BF16), ((SIDE * rows + TAIL, width), BF16), ((8, LANES), F32)],
        [log_scale, bias],
        pair_near + column_near,
        1,
        24 * rows * width,
    )
    pairs_in = [pair_all] + [send(pair_all, pair_step(step)) for step in STEPS]
    columns_in = [column_all, send(column_all, column_move)]
    pairs_sib = [send(block, to_sibling) for block in pairs_in]
    columns_sib = [send(block, to_sibling) for block in columns_in]
    half = 4 * tall * tall * width
    flat = (tall, width)
    sums_shape = ((3, 8, LANES), F32)

    def images_kept(count):
        return [pltpu.VMEM((count, width), BF16), pltpu.VMEM((count, LANES), F32)]

    shared = [((2 * tall, tall), BF16), ((2 * tall, width), BF16)]
    own_grad, coef, weighted, own_sums, txt_all = call(
        own_kernel,
        [(flat, F32)] + shared + [sums_shape, (flat, BF16)],
        [],
        [given] + pairs_in + columns_in,
        half,
        16 * tall * width,
        images_kept(tall),
        VMEM_MIB,
    )
    moved, sums = [], [own_sums]
    for chip in range(2):
        count = tall // 2
        sib_grad, coef, weighted, sib_sums = call(
            functools.partial(sibling_kernel, chip),
            [((count, width), F32)] + shared + [sums_shape],
            [],
            [given] + pairs_sib + [columns_sib[chip], txt_all, coef, weighted],
            half // 2,
            8 * tall * width,
            images_kept(count),
            VMEM_MIB,
            {7: 1, 8: 2},
        )
        moved.append(send(sib_grad, to_sibling))
        sums.append(sib_sums)
    near_txt, far_txt, sums = call(
        text_kernel,
        [((SIDE * rows, width), F32)] * 2 + [((devices, LANES), F32)],
        [],
        sums + [weight_row, coef, weighted],
        half,
        12 * tall * width,
        (),
        VMEM_MIB,
    )
    pair_keep, pair_send, column_keep, column_send = call(
        merge_kernel,
        [
            ((span, width), F32),
            ((SIDE - 1, span, width), F32),
            ((SIDE * rows, width), F32),
            ((SIDE * rows, width), F32),
        ],
        [],
        [own_grad] + moved + [near_txt, far_txt],
        1,
        24 * tall * width,
    )
    column_sum = column_keep + send(column_send.astype(SEND), column_move).astype(F32)
    pair_sum = pair_keep
    for index, step in enumerate(STEPS):
        pair_sum = pair_sum + send(pair_send[index].astype(SEND), pair_step(-step)).astype(F32)
    all_sums = lax.all_to_all(sums, AXES, 0, 0, tiled=True)
    pair_last = pair_sum[:rows] + send(pair_sum[rows:].astype(SEND), pair_move).astype(F32)
    column_last = column_sum[:rows]
    for index, step in enumerate(STEPS):
        block = column_sum[(index + 1) * rows : (index + 2) * rows]
        column_last = column_last + send(block.astype(SEND), column_step(-step)).astype(F32)
    grad_image, grad_text, scalars = call(
        finish_kernel,
        [((rows, width), F32), ((rows, width), F32), ((3,), F32)],
        [],
        [given, all_sums, image_embeds, text_embeds, weight_row, pair_last, column_last],
        2 * 12 * rows * width,
        24 * rows * width,
    )
    return grad_image, grad_text, scalars


def solution(mesh):
    placed = (P(AXES, None), P(AXES, None), P(AXES), P(), P())
    return jax.shard_map(
        body,
        mesh=mesh,
        in_specs=placed,
        out_specs=(P(AXES, None), P(AXES, None), P()),
        check_vma=False,
    )
```

```python
import functools

import jax
import jax.numpy as jnp
from jax import lax
from jax.experimental import pallas as pl
from jax.experimental.pallas import tpu as pltpu
from jax.sharding import PartitionSpec as P

F32 = jnp.float32
BF16 = jnp.bfloat16
SEND = jnp.float16
SIDE = 4
AXES = ("blk", "group")
LANES = 128
LOG2_E = 1.4426950408889634
TAIL = 16
CONTRACT_LAST = (((1,), (1,)), ((), ()))
CONTRACT_FIRST = (((0,), (0,)), ((), ()))


def place(x, y, z, core):
    return (y * 2 + x % 2) * 16 + (z * 2 + x // 2) * 2 + core


def pairs(move):
    found = []
    for x in range(SIDE):
        for y in range(SIDE):
            for z in range(SIDE):
                for core in range(2):
                    found.append((place(x, y, z, core), place(*move(x, y, z, core))))
    return found


def send(values, move):
    return lax.ppermute(values, AXES, pairs(move))


def pair_move(x, y, z, core):
    return (x ^ 1 if core == 0 else 3 - x, y, z, core)


def column_move(x, y, z, core):
    return (3 - x if core == 0 else x ^ 1, y, z, core)


def to_sibling(x, y, z, core):
    return (x, y, z, 1 - core)


def pair_step(step):
    return lambda x, y, z, core: (
        (x, y, (z + step) % SIDE, core) if core == 0 else (x, (y + step) % SIDE, z, core)
    )


def column_step(step):
    return lambda x, y, z, core: (
        (x, (y + step) % SIDE, z, core) if core == 0 else (x, y, (z + step) % SIDE, core)
    )


STEPS = (2, 3, 1)


def on_core():
    return lax.rem(lax.axis_index("group"), 2)


def row_norm_of(wide):
    return jnp.sqrt(jnp.sum(wide * wide, axis=1, keepdims=True) + 1e-06)


def column_of(weight_row, width):
    return jnp.transpose(jnp.broadcast_to(weight_row, (width, weight_row.shape[1])))


def prepare_kernel(img_ref, txt_ref, wgt_ref, pair_out, column_out):
    rows, width = img_ref.shape
    img = img_ref[...].astype(F32)
    img = (img / row_norm_of(img)).astype(BF16)
    txt = txt_ref[...].astype(F32)
    txt = (txt / row_norm_of(txt)).astype(BF16)
    here = pl.ds(0, rows)
    for out in (pair_out, column_out):
        out[pl.ds(rows, TAIL), :] = jnp.zeros((TAIL, width), BF16)
        out[pl.ds(rows, TAIL), pl.ds(0, rows)] = jnp.broadcast_to(wgt_ref[...], (TAIL, rows))

    @pl.when(on_core() == 0)
    def _():
        pair_out[here, :] = img
        column_out[here, :] = txt

    @pl.when(on_core() == 1)
    def _():
        pair_out[here, :] = txt
        column_out[here, :] = img


def join_kernel(log_scale_ref, bias_ref, *refs):
    pair_refs, column_refs, (pair_out, column_out, given) = refs[:2], refs[2:6], refs[6:]
    given[0:1, :] = jnp.exp(jnp.full((1, LANES), log_scale_ref[0], F32))
    given[1:2, :] = jnp.full((1, LANES), bias_ref[0], F32)
    for blocks, out in ((pair_refs, pair_out), (column_refs, column_out)):
        rows = blocks[0].shape[0] - TAIL
        tail = pl.ds(len(blocks) * rows, TAIL)
        out[tail, :] = jnp.zeros((TAIL, out.shape[1]), BF16)
        for index, block in enumerate(blocks):
            out[pl.ds(index * rows, rows), :] = block[pl.ds(0, rows), :]
            out[tail, pl.ds(index * rows, rows)] = block[pl.ds(rows, TAIL), pl.ds(0, rows)]


def weights_of(block, rows, first):
    return block[pl.ds(2 * rows, TAIL), :][0:1, first : first + rows].astype(F32)


def take_pairs(blocks, rows_out, wgt_out):
    rows = rows_out.shape[0] // (2 * SIDE)
    for step, block in enumerate(blocks):
        for chip in range(2):
            there = pl.ds((chip * SIDE + step) * rows, rows)
            rows_out[there, :] = block[pl.ds(chip * rows, rows), :]
            if wgt_out is not None:
                wgt_out[there, :] = column_of(weights_of(block, rows, chip * rows), LANES)


def take_columns(blocks, rows_out, wgt_out):
    span = rows_out.shape[0] // len(blocks)
    for index, block in enumerate(blocks):
        there = pl.ds(index * span, span)
        rows_out[there, :] = block[pl.ds(0, span), :]
        if wgt_out is not None:
            weight = block[pl.ds(span, TAIL), :][0:1, :span].astype(F32)
            wgt_out[there, :] = column_of(weight, LANES)


def score_part(img_all, wgt_all, txt_all, scale, bias, first, coef_out, weighted_out, grad_out, sums_out):
    count, width = img_all.shape
    scale_two, bias_two = scale * LOG2_E, bias * LOG2_E
    span = 256
    rows = 128
    zero = jnp.zeros((8, LANES), F32)
    loss, diff, score = zero, zero, zero
    same = lax.broadcasted_iota(jnp.int32, (rows, LANES), 0) == lax.broadcasted_iota(
        jnp.int32, (rows, LANES), 1
    )

    def fold(values):
        return jnp.sum(values.reshape(-1, 8, LANES), axis=0)

    def scores_of(part):
        img = img_all[pl.ds(span * part, span), :]
        return lax.dot_general(img, txt_all[...], CONTRACT_LAST, preferred_element_type=F32)

    def gradient_of(part):
        here = pl.ds(span * part, span)
        there = pl.ds(first + span * part, span)
        grad_out[here, :] = jnp.dot(coef_out[there, :], txt_all[...], preferred_element_type=F32)

    parts = count // span
    scores = scores_of(0)
    for part in range(parts):
        next_scores = scores_of(part + 1) if part + 1 < parts else None
        if part:
            gradient_of(part - 1)
        here = pl.ds(span * part, span)
        there = pl.ds(first + span * part, span)
        weight = wgt_all[here, :]
        weighted_out[there, :] = (
            img_all[here, :].astype(F32) * jnp.tile(weight, (1, width // LANES))
        ).astype(BF16)
        for tile in range(scores.shape[1] // LANES):
            score_tile = scores[:, tile * LANES : (tile + 1) * LANES]
            grown = jnp.exp2(score_tile * scale_two + bias_two)
            beyond = 1.0 + grown
            diffs = grown / beyond
            if first == 0 and part == 0 and tile == 0:
                diffs = jnp.concatenate(
                    [jnp.where(same, diffs[:rows] - 1.0, diffs[:rows]), diffs[rows:]], axis=0
                )
                matched = jnp.where(same, score_tile[:rows] * scale + bias, 0.0)
                loss = loss - fold(matched * weight[:rows])
            coef_out[there, pl.ds(tile * LANES, LANES)] = diffs.astype(BF16)
            if tile == 0:
                over, diff_row, score_row = grown, diffs, diffs * score_tile
            else:
                over = over * beyond + grown
                diff_row = diff_row + diffs
                score_row = score_row + diffs * score_tile
        loss = loss + fold(jnp.log1p(over) * weight)
        diff = diff + fold(diff_row * weight)
        score = score + fold(score_row * weight)
        scores = next_scores
    gradient_of(parts - 1)
    sums_out[0] = loss
    sums_out[1] = score
    sums_out[2] = diff


def own_kernel(given, *refs):
    pair_refs, column_refs = refs[:4], refs[4:6]
    grad_out, coef_out, weighted_out, sums_out, txt_all, img_all, wgt_all = refs[6:]

    @pl.when(on_core() == 0)
    def _():
        take_pairs(pair_refs, img_all, wgt_all)
        take_columns(column_refs, txt_all, None)

    @pl.when(on_core() == 1)
    def _():
        take_columns(column_refs, img_all, wgt_all)
        take_pairs(pair_refs, txt_all, None)

    score_part(
        img_all, wgt_all, txt_all, given[0:1, :], given[1:2, :], 0, coef_out, weighted_out, grad_out, sums_out
    )


def sibling_kernel(chip, given, *refs):
    pair_refs, column_ref, txt_all = refs[:4], refs[4], refs[5]
    grad_out, coef_out, weighted_out, sums_out, img_all, wgt_all = refs[8:]
    span = img_all.shape[0]
    rows = span // SIDE

    @pl.when(on_core() == 0)
    def _():
        take_columns((column_ref,), img_all, wgt_all)

    @pl.when(on_core() == 1)
    def _():
        for step, block in enumerate(pair_refs):
            there = pl.ds(step * rows, rows)
            img_all[there, :] = block[pl.ds(chip * rows, rows), :]
            wgt_all[there, :] = column_of(weights_of(block, rows, chip * rows), LANES)

    score_part(
        img_all, wgt_all, txt_all, given[0:1, :], given[1:2, :], (2 + chip) * span, coef_out, weighted_out, grad_out, sums_out
    )


def text_kernel(*refs):
    sums_refs, wgt_ref, coef, weighted = refs[:3], *refs[3:6]
    near_out, far_out, sums_out = refs[6:]
    span = near_out.shape[0]
    for chip, out in enumerate((near_out, far_out)):
        here = pl.ds(chip * span, span)
        out[...] = lax.dot_general(
            coef[:, here], weighted[...], CONTRACT_FIRST, preferred_element_type=F32
        )
    lane = lax.broadcasted_iota(jnp.int32, (1, LANES), 1)
    row = jnp.where(lane == 3, jnp.sum(wgt_ref[...].astype(F32), axis=1, keepdims=True), 0.0)
    for kind in range(3):
        part = jnp.sum(sum(ref[kind] for ref in sums_refs), axis=0, keepdims=True)
        row = row + jnp.where(lane == kind, jnp.sum(part, axis=1, keepdims=True), 0.0)
    sums_out[...] = jnp.broadcast_to(row, sums_out.shape)


def merge_kernel(own_grad, near_moved, far_moved, near_txt, far_txt, *outs):
    pair_keep, pair_send, column_keep, column_send = outs
    span = near_txt.shape[0]
    rows = span // SIDE

    def put_pair(chip, step, values):
        there = pl.ds(chip * rows, rows)
        if step == 0:
            pair_keep[there, :] = values
        else:
            pair_send[step - 1, there, :] = values

    for chip, (moved, txt, column) in enumerate(
        ((near_moved, near_txt, column_keep), (far_moved, far_txt, column_send))
    ):
        for step in range(SIDE):
            here = pl.ds(step * rows, rows)
            img_here = pl.ds(chip * span + step * rows, rows)

            @pl.when(on_core() == 0)
            def _():
                put_pair(chip, step, own_grad[img_here, :] + moved[here, :])
                column[here, :] = txt[here, :]

            @pl.when(on_core() == 1)
            def _():
                put_pair(chip, step, txt[here, :])
                column[here, :] = own_grad[img_here, :] + moved[here, :]


def back_kernel(given, img_ref, txt_ref, wgt_ref, pair_sum, column_sum, img_out, txt_out):
    rows, width = img_ref.shape
    pair_count = float(rows * 2 * SIDE**3)
    scale = jnp.tile(given[0:1, :], (1, width // LANES))
    first = on_core() == 0

    def back(gradient, values):
        norm = row_norm_of(values)
        unit = values / norm
        inner = jnp.sum(unit * gradient, axis=1, keepdims=True)
        return pair_count * (gradient - unit * inner) / norm

    weight = jnp.tile(column_of(wgt_ref[...].astype(F32), LANES), (1, width // LANES))
    img_sum = jnp.where(first, pair_sum[...], column_sum[...])
    txt_sum = jnp.where(first, column_sum[...], pair_sum[...])
    img_out[...] = back(scale * weight * img_sum, img_ref[...].astype(F32))
    txt_out[...] = back(scale * txt_sum, txt_ref[...].astype(F32))


def finish_kernel(given, sums_ref, img_back, txt_back, img_out, txt_out, scalar_out):
    lane = lax.broadcasted_iota(jnp.int32, (1, LANES), 1)
    sums = jnp.sum(sums_ref[...], axis=0, keepdims=True)
    total = jnp.sum(jnp.where(lane == 3, sums, 0.0), axis=1, keepdims=True)
    share = 1.0 / total
    img_out[...] = img_back[...] * share
    txt_out[...] = txt_back[...] * share
    ratio = jnp.where(lane == 1, given[0:1, :], 1.0) * sums / total
    for kind in range(3):
        scalar_out[kind] = jnp.sum(jnp.where(lane == kind, ratio, 0.0))


VMEM_MIB = 24
LONG_FLOPS = 4 * 10**10
IN_VMEM = pl.BlockSpec(memory_space=pltpu.VMEM)
IN_SMEM = pl.BlockSpec(memory_space=pltpu.SMEM)


def call(kernel, shapes, scalars, arrays, flops, moved, scratch=(), limit=16, aliases=None):
    return pl.pallas_call(
        kernel,
        out_shape=[jax.ShapeDtypeStruct(shape, kind) for shape, kind in shapes],
        in_specs=[IN_SMEM] * len(scalars) + [IN_VMEM] * len(arrays),
        out_specs=[IN_SMEM if len(shape) == 1 else IN_VMEM for shape, kind in shapes],
        scratch_shapes=list(scratch),
        input_output_aliases=aliases or {},
        compiler_params=pltpu.CompilerParams(vmem_limit_bytes=limit * 2**20),
        cost_estimate=pl.CostEstimate(flops=flops, bytes_accessed=moved, transcendentals=0),
    )(*scalars, *arrays)


def body(image_embeds, text_embeds, pair_weights, log_scale, bias):
    rows, width = image_embeds.shape
    span, tall = 2 * rows, 2 * SIDE * rows
    devices = 2 * SIDE**3
    weight_row = pair_weights.reshape(1, rows)
    pair_own, column_own = call(
        prepare_kernel,
        [((rows + TAIL, width), BF16)] * 2,
        [],
        [image_embeds, text_embeds, weight_row],
        2 * 8 * rows * width,
        8 * rows * width,
    )
    column_near = [column_own] + [send(column_own, column_step(step)) for step in STEPS]
    pair_near = [pair_own, send(pair_own, pair_move)]
    pair_all, column_all, given = call(
        join_kernel,
        [((span + TAIL, width), BF16), ((SIDE * rows + TAIL, width), BF16), ((8, LANES), F32)],
        [log_scale, bias],
        pair_near + column_near,
        1,
        24 * rows * width,
    )
    pairs_in = [pair_all] + [send(pair_all, pair_step(step)) for step in STEPS]
    columns_in = [column_all, send(column_all, column_move)]
    pairs_sib = [send(block, to_sibling) for block in pairs_in]
    columns_sib = [send(block, to_sibling) for block in columns_in]
    half = 4 * tall * tall * width
    flat = (tall, width)
    sums_shape = ((3, 8, LANES), F32)

    def images_kept(count):
        return [pltpu.VMEM((count, width), BF16), pltpu.VMEM((count, LANES), F32)]

    shared = [((2 * tall, tall), BF16), ((2 * tall, width), BF16)]
    own_grad, coef, weighted, own_sums, txt_all = call(
        own_kernel,
        [(flat, F32)] + shared + [sums_shape, (flat, BF16)],
        [],
        [given] + pairs_in + columns_in,
        half,
        16 * tall * width,
        images_kept(tall),
        VMEM_MIB,
    )
    moved, sums = [], [own_sums]
    for chip in range(2):
        count = tall // 2
        sib_grad, coef, weighted, sib_sums = call(
            functools.partial(sibling_kernel, chip),
            [((count, width), F32)] + shared + [sums_shape],
            [],
            [given] + pairs_sib + [columns_sib[chip], txt_all, coef, weighted],
            half // 2,
            8 * tall * width,
            images_kept(count),
            VMEM_MIB,
            {7: 1, 8: 2},
        )
        moved.append(send(sib_grad, to_sibling))
        sums.append(sib_sums)
    near_txt, far_txt, sums = call(
        text_kernel,
        [((SIDE * rows, width), F32)] * 2 + [((devices, LANES), F32)],
        [],
        sums + [weight_row, coef, weighted],
        half,
        12 * tall * width,
        (),
        VMEM_MIB,
    )
    pair_keep, pair_send, column_keep, column_send = call(
        merge_kernel,
        [
            ((span, width), F32),
            ((SIDE - 1, span, width), F32),
            ((SIDE * rows, width), F32),
            ((SIDE * rows, width), F32),
        ],
        [],
        [own_grad] + moved + [near_txt, far_txt],
        1,
        24 * tall * width,
    )
    column_sum = column_keep + send(column_send.astype(SEND), column_move).astype(F32)
    pair_sum = pair_keep + 0.0 * column_sum[0, 0]
    for index, step in enumerate(STEPS):
        pair_sum = pair_sum + send(pair_send[index].astype(SEND), pair_step(-step)).astype(F32)
    all_sums = lax.all_to_all(sums, AXES, 0, 0, tiled=True)
    pair_last = pair_sum[:rows] + send(pair_sum[rows:].astype(SEND), pair_move).astype(F32)
    column_last = column_sum[:rows]
    for index, step in enumerate(STEPS):
        block = column_sum[(index + 1) * rows : (index + 2) * rows]
        column_last = column_last + send(block.astype(SEND), column_step(-step)).astype(F32)
    img_back, txt_back = call(
        back_kernel,
        [((rows, width), F32)] * 2,
        [],
        [given, image_embeds, text_embeds, weight_row, pair_last, column_last],
        LONG_FLOPS,
        24 * rows * width,
    )
    grad_image, grad_text, scalars = call(
        finish_kernel,
        [((rows, width), F32), ((rows, width), F32), ((3,), F32)],
        [],
        [given, all_sums, img_back, txt_back],
        2 * rows * width,
        16 * rows * width,
    )
    return grad_image, grad_text, scalars


def solution(mesh):
    placed = (P(AXES, None), P(AXES, None), P(AXES), P(), P())
    return jax.shard_map(
        body,
        mesh=mesh,
        in_specs=placed,
        out_specs=(P(AXES, None), P(AXES, None), P()),
        check_vma=False,
    )
```

```python
import functools

import jax
import jax.numpy as jnp
from jax import lax
from jax.experimental import pallas as pl
from jax.experimental.pallas import tpu as pltpu
from jax.sharding import PartitionSpec as P

F32 = jnp.float32
BF16 = jnp.bfloat16
SEND = jnp.float16
SIDE = 4
AXES = ("blk", "group")
LANES = 128
LOG2_E = 1.4426950408889634
TAIL = 16
CONTRACT_LAST = (((1,), (1,)), ((), ()))
CONTRACT_FIRST = (((0,), (0,)), ((), ()))


def place(x, y, z, core):
    return (y * 2 + x % 2) * 16 + (z * 2 + x // 2) * 2 + core


def pairs(move):
    found = []
    for x in range(SIDE):
        for y in range(SIDE):
            for z in range(SIDE):
                for core in range(2):
                    found.append((place(x, y, z, core), place(*move(x, y, z, core))))
    return found


def send(values, move):
    return lax.ppermute(values, AXES, pairs(move))


def pair_move(x, y, z, core):
    return (x ^ 1 if core == 0 else 3 - x, y, z, core)


def column_move(x, y, z, core):
    return (3 - x if core == 0 else x ^ 1, y, z, core)


def to_sibling(x, y, z, core):
    return (x, y, z, 1 - core)


def pair_step(step):
    return lambda x, y, z, core: (
        (x, y, (z + step) % SIDE, core) if core == 0 else (x, (y + step) % SIDE, z, core)
    )


def column_step(step):
    return lambda x, y, z, core: (
        (x, (y + step) % SIDE, z, core) if core == 0 else (x, y, (z + step) % SIDE, core)
    )


STEPS = (2, 3, 1)


def on_core():
    return lax.rem(lax.axis_index("group"), 2)


def row_norm_of(wide):
    return jnp.sqrt(jnp.sum(wide * wide, axis=1, keepdims=True) + 1e-06)


def column_of(weight_row, width):
    return jnp.transpose(jnp.broadcast_to(weight_row, (width, weight_row.shape[1])))


def prepare_kernel(img_ref, txt_ref, wgt_ref, pair_out, column_out):
    rows, width = img_ref.shape
    img = img_ref[...].astype(F32)
    img = (img / row_norm_of(img)).astype(BF16)
    txt = txt_ref[...].astype(F32)
    txt = (txt / row_norm_of(txt)).astype(BF16)
    here = pl.ds(0, rows)
    for out in (pair_out, column_out):
        out[pl.ds(rows, TAIL), :] = jnp.zeros((TAIL, width), BF16)
        out[pl.ds(rows, TAIL), pl.ds(0, rows)] = jnp.broadcast_to(wgt_ref[...], (TAIL, rows))

    @pl.when(on_core() == 0)
    def _():
        pair_out[here, :] = img
        column_out[here, :] = txt

    @pl.when(on_core() == 1)
    def _():
        pair_out[here, :] = txt
        column_out[here, :] = img


def join_kernel(log_scale_ref, bias_ref, *refs):
    pair_refs, column_refs, (pair_out, column_out, given) = refs[:2], refs[2:6], refs[6:]
    given[0:1, :] = jnp.exp(jnp.full((1, LANES), log_scale_ref[0], F32))
    given[1:2, :] = jnp.full((1, LANES), bias_ref[0], F32)
    for blocks, out in ((pair_refs, pair_out), (column_refs, column_out)):
        rows = blocks[0].shape[0] - TAIL
        tail = pl.ds(len(blocks) * rows, TAIL)
        out[tail, :] = jnp.zeros((TAIL, out.shape[1]), BF16)
        for index, block in enumerate(blocks):
            out[pl.ds(index * rows, rows), :] = block[pl.ds(0, rows), :]
            out[tail, pl.ds(index * rows, rows)] = block[pl.ds(rows, TAIL), pl.ds(0, rows)]


def weights_of(block, rows, first):
    return block[pl.ds(2 * rows, TAIL), :][0:1, first : first + rows].astype(F32)


def take_pairs(blocks, rows_out, wgt_out):
    rows = rows_out.shape[0] // (2 * SIDE)
    for step, block in enumerate(blocks):
        for chip in range(2):
            there = pl.ds((chip * SIDE + step) * rows, rows)
            rows_out[there, :] = block[pl.ds(chip * rows, rows), :]
            if wgt_out is not None:
                wgt_out[there, :] = column_of(weights_of(block, rows, chip * rows), LANES)


def take_columns(blocks, rows_out, wgt_out):
    span = rows_out.shape[0] // len(blocks)
    for index, block in enumerate(blocks):
        there = pl.ds(index * span, span)
        rows_out[there, :] = block[pl.ds(0, span), :]
        if wgt_out is not None:
            weight = block[pl.ds(span, TAIL), :][0:1, :span].astype(F32)
            wgt_out[there, :] = column_of(weight, LANES)


def score_part(img_all, wgt_all, txt_all, scale, bias, first, coef_out, weighted_out, grad_out, sums_out):
    count, width = img_all.shape
    scale_two, bias_two = scale * LOG2_E, bias * LOG2_E
    span = 256
    rows = 128
    zero = jnp.zeros((8, LANES), F32)
    loss, diff, score = zero, zero, zero
    same = lax.broadcasted_iota(jnp.int32, (rows, LANES), 0) == lax.broadcasted_iota(
        jnp.int32, (rows, LANES), 1
    )

    def fold(values):
        return jnp.sum(values.reshape(-1, 8, LANES), axis=0)

    def scores_of(part):
        img = img_all[pl.ds(span * part, span), :]
        return lax.dot_general(img, txt_all[...], CONTRACT_LAST, preferred_element_type=F32)

    def gradient_of(part):
        here = pl.ds(span * part, span)
        there = pl.ds(first + span * part, span)
        grad_out[here, :] = jnp.dot(coef_out[there, :], txt_all[...], preferred_element_type=F32)

    parts = count // span
    scores = scores_of(0)
    for part in range(parts):
        next_scores = scores_of(part + 1) if part + 1 < parts else None
        if part:
            gradient_of(part - 1)
        here = pl.ds(span * part, span)
        there = pl.ds(first + span * part, span)
        weight = wgt_all[here, :]
        weighted_out[there, :] = (
            img_all[here, :].astype(F32) * jnp.tile(weight, (1, width // LANES))
        ).astype(BF16)
        for tile in range(scores.shape[1] // LANES):
            score_tile = scores[:, tile * LANES : (tile + 1) * LANES]
            grown = jnp.exp2(score_tile * scale_two + bias_two)
            beyond = 1.0 + grown
            diffs = grown / beyond
            if first == 0 and part == 0 and tile == 0:
                diffs = jnp.concatenate(
                    [jnp.where(same, diffs[:rows] - 1.0, diffs[:rows]), diffs[rows:]], axis=0
                )
                matched = jnp.where(same, score_tile[:rows] * scale + bias, 0.0)
                loss = loss - fold(matched * weight[:rows])
            coef_out[there, pl.ds(tile * LANES, LANES)] = diffs.astype(BF16)
            if tile == 0:
                over, diff_row, score_row = grown, diffs, diffs * score_tile
            else:
                over = over * beyond + grown
                diff_row = diff_row + diffs
                score_row = score_row + diffs * score_tile
        loss = loss + fold(jnp.log1p(over) * weight)
        diff = diff + fold(diff_row * weight)
        score = score + fold(score_row * weight)
        scores = next_scores
    gradient_of(parts - 1)
    sums_out[0] = loss
    sums_out[1] = score
    sums_out[2] = diff


def own_kernel(given, *refs):
    pair_refs, column_refs = refs[:4], refs[4:6]
    grad_out, coef_out, weighted_out, sums_out, txt_all, img_all, wgt_all = refs[6:]

    @pl.when(on_core() == 0)
    def _():
        take_pairs(pair_refs, img_all, wgt_all)
        take_columns(column_refs, txt_all, None)

    @pl.when(on_core() == 1)
    def _():
        take_columns(column_refs, img_all, wgt_all)
        take_pairs(pair_refs, txt_all, None)

    score_part(
        img_all, wgt_all, txt_all, given[0:1, :], given[1:2, :], 0, coef_out, weighted_out, grad_out, sums_out
    )


def sibling_kernel(chip, given, *refs):
    pair_refs, column_ref, txt_all = refs[:4], refs[4], refs[5]
    grad_out, coef_out, weighted_out, sums_out, img_all, wgt_all = refs[8:]
    span = img_all.shape[0]
    rows = span // SIDE

    @pl.when(on_core() == 0)
    def _():
        take_columns((column_ref,), img_all, wgt_all)

    @pl.when(on_core() == 1)
    def _():
        for step, block in enumerate(pair_refs):
            there = pl.ds(step * rows, rows)
            img_all[there, :] = block[pl.ds(chip * rows, rows), :]
            wgt_all[there, :] = column_of(weights_of(block, rows, chip * rows), LANES)

    score_part(
        img_all, wgt_all, txt_all, given[0:1, :], given[1:2, :], (2 + chip) * span, coef_out, weighted_out, grad_out, sums_out
    )


def text_kernel(*refs):
    sums_refs, wgt_ref, coef, weighted = refs[:3], *refs[3:6]
    near_out, far_out, sums_out = refs[6:]
    span = near_out.shape[0]
    for chip, out in enumerate((near_out, far_out)):
        here = pl.ds(chip * span, span)
        out[...] = lax.dot_general(
            coef[:, here], weighted[...], CONTRACT_FIRST, preferred_element_type=F32
        )
    lane = lax.broadcasted_iota(jnp.int32, (1, LANES), 1)
    row = jnp.where(lane == 3, jnp.sum(wgt_ref[...].astype(F32), axis=1, keepdims=True), 0.0)
    for kind in range(3):
        part = jnp.sum(sum(ref[kind] for ref in sums_refs), axis=0, keepdims=True)
        row = row + jnp.where(lane == kind, jnp.sum(part, axis=1, keepdims=True), 0.0)
    sums_out[...] = jnp.broadcast_to(row, sums_out.shape)


def merge_kernel(own_grad, near_moved, far_moved, near_txt, far_txt, *outs):
    pair_keep, pair_send, column_keep, column_send = outs
    span = near_txt.shape[0]
    rows = span // SIDE

    def put_pair(chip, step, values):
        there = pl.ds(chip * rows, rows)
        if step == 0:
            pair_keep[there, :] = values
        else:
            pair_send[step - 1, there, :] = values

    for chip, (moved, txt, column) in enumerate(
        ((near_moved, near_txt, column_keep), (far_moved, far_txt, column_send))
    ):
        for step in range(SIDE):
            here = pl.ds(step * rows, rows)
            img_here = pl.ds(chip * span + step * rows, rows)

            @pl.when(on_core() == 0)
            def _():
                put_pair(chip, step, own_grad[img_here, :] + moved[here, :])
                column[here, :] = txt[here, :]

            @pl.when(on_core() == 1)
            def _():
                put_pair(chip, step, txt[here, :])
                column[here, :] = own_grad[img_here, :] + moved[here, :]


def back_kernel(given, img_ref, txt_ref, wgt_ref, pair_sum, column_sum, img_out, txt_out):
    rows, width = img_ref.shape
    pair_count = float(rows * 2 * SIDE**3)
    scale = jnp.tile(given[0:1, :], (1, width // LANES))
    first = on_core() == 0

    def back(gradient, values):
        norm = row_norm_of(values)
        unit = values / norm
        inner = jnp.sum(unit * gradient, axis=1, keepdims=True)
        return pair_count * (gradient - unit * inner) / norm

    weight = jnp.tile(column_of(wgt_ref[...].astype(F32), LANES), (1, width // LANES))
    img_sum = jnp.where(first, pair_sum[...], column_sum[...])
    txt_sum = jnp.where(first, column_sum[...], pair_sum[...])
    img_out[...] = back(scale * weight * img_sum, img_ref[...].astype(F32))
    txt_out[...] = back(scale * txt_sum, txt_ref[...].astype(F32))


def finish_kernel(given, sums_ref, img_back, txt_back, img_out, txt_out, scalar_out):
    lane = lax.broadcasted_iota(jnp.int32, (1, LANES), 1)
    sums = jnp.sum(sums_ref[...], axis=0, keepdims=True)
    total = jnp.sum(jnp.where(lane == 3, sums, 0.0), axis=1, keepdims=True)
    share = 1.0 / total
    img_out[...] = img_back[...] * share
    txt_out[...] = txt_back[...] * share
    ratio = jnp.where(lane == 1, given[0:1, :], 1.0) * sums / total
    for kind in range(3):
        scalar_out[kind] = jnp.sum(jnp.where(lane == kind, ratio, 0.0))


VMEM_MIB = 24
LONG_FLOPS = 4 * 10**10
IN_VMEM = pl.BlockSpec(memory_space=pltpu.VMEM)
IN_SMEM = pl.BlockSpec(memory_space=pltpu.SMEM)


def call(kernel, shapes, scalars, arrays, flops, moved, scratch=(), limit=16, aliases=None):
    return pl.pallas_call(
        kernel,
        out_shape=[jax.ShapeDtypeStruct(shape, kind) for shape, kind in shapes],
        in_specs=[IN_SMEM] * len(scalars) + [IN_VMEM] * len(arrays),
        out_specs=[IN_SMEM if len(shape) == 1 else IN_VMEM for shape, kind in shapes],
        scratch_shapes=list(scratch),
        input_output_aliases=aliases or {},
        compiler_params=pltpu.CompilerParams(vmem_limit_bytes=limit * 2**20),
        cost_estimate=pl.CostEstimate(flops=flops, bytes_accessed=moved, transcendentals=0),
    )(*scalars, *arrays)


def body(image_embeds, text_embeds, pair_weights, log_scale, bias):
    rows, width = image_embeds.shape
    span, tall = 2 * rows, 2 * SIDE * rows
    devices = 2 * SIDE**3
    weight_row = pair_weights.reshape(1, rows)
    pair_own, column_own = call(
        prepare_kernel,
        [((rows + TAIL, width), BF16)] * 2,
        [],
        [image_embeds, text_embeds, weight_row],
        2 * 8 * rows * width,
        8 * rows * width,
    )
    column_near = [column_own] + [send(column_own, column_step(step)) for step in STEPS]
    pair_near = [pair_own, send(pair_own, pair_move)]
    pair_all, column_all, given = call(
        join_kernel,
        [((span + TAIL, width), BF16), ((SIDE * rows + TAIL, width), BF16), ((8, LANES), F32)],
        [log_scale, bias],
        pair_near + column_near,
        1,
        24 * rows * width,
    )
    pairs_in = [pair_all] + [send(pair_all, pair_step(step)) for step in STEPS]
    columns_in = [column_all, send(column_all, column_move)]
    pairs_sib = [send(block, to_sibling) for block in pairs_in]
    columns_sib = [send(block, to_sibling) for block in columns_in]
    half = 4 * tall * tall * width
    flat = (tall, width)
    sums_shape = ((3, 8, LANES), F32)

    def images_kept(count):
        return [pltpu.VMEM((count, width), BF16), pltpu.VMEM((count, LANES), F32)]

    shared = [((2 * tall, tall), BF16), ((2 * tall, width), BF16)]
    own_grad, coef, weighted, own_sums, txt_all = call(
        own_kernel,
        [(flat, F32)] + shared + [sums_shape, (flat, BF16)],
        [],
        [given] + pairs_in + columns_in,
        half,
        16 * tall * width,
        images_kept(tall),
        VMEM_MIB,
    )
    moved, sums = [], [own_sums]
    for chip in range(2):
        count = tall // 2
        sib_grad, coef, weighted, sib_sums = call(
            functools.partial(sibling_kernel, chip),
            [((count, width), F32)] + shared + [sums_shape],
            [],
            [given] + pairs_sib + [columns_sib[chip], txt_all, coef, weighted],
            half // 2,
            8 * tall * width,
            images_kept(count),
            VMEM_MIB,
            {7: 1, 8: 2},
        )
        moved.append(send(sib_grad, to_sibling))
        sums.append(sib_sums)
    near_txt, far_txt, sums = call(
        text_kernel,
        [((SIDE * rows, width), F32)] * 2 + [((devices, LANES), F32)],
        [],
        sums + [weight_row, coef, weighted],
        half,
        12 * tall * width,
        (),
        VMEM_MIB,
    )
    pair_keep, pair_send, column_keep, column_send = call(
        merge_kernel,
        [
            ((span, width), F32),
            ((SIDE - 1, span, width), F32),
            ((SIDE * rows, width), F32),
            ((SIDE * rows, width), F32),
        ],
        [],
        [own_grad] + moved + [near_txt, far_txt],
        1,
        24 * tall * width,
    )
    column_sum = column_keep + send(column_send.astype(SEND), column_move).astype(F32)
    pair_sum = pair_keep + 0.0 * column_sum[:span]
    for index, step in enumerate(STEPS):
        pair_sum = pair_sum + send(pair_send[index].astype(SEND), pair_step(-step)).astype(F32)
    all_sums = lax.all_to_all(sums, AXES, 0, 0, tiled=True)
    pair_last = pair_sum[:rows] + send(pair_sum[rows:].astype(SEND), pair_move).astype(F32)
    column_last = column_sum[:rows]
    for index, step in enumerate(STEPS):
        block = column_sum[(index + 1) * rows : (index + 2) * rows]
        column_last = column_last + send(block.astype(SEND), column_step(-step)).astype(F32)
    img_back, txt_back = call(
        back_kernel,
        [((rows, width), F32)] * 2,
        [],
        [given, image_embeds, text_embeds, weight_row, pair_last, column_last],
        LONG_FLOPS,
        24 * rows * width,
    )
    grad_image, grad_text, scalars = call(
        finish_kernel,
        [((rows, width), F32), ((rows, width), F32), ((3,), F32)],
        [],
        [given, all_sums, img_back, txt_back],
        2 * rows * width,
        16 * rows * width,
    )
    return grad_image, grad_text, scalars


def solution(mesh):
    placed = (P(AXES, None), P(AXES, None), P(AXES), P(), P())
    return jax.shard_map(
        body,
        mesh=mesh,
        in_specs=placed,
        out_specs=(P(AXES, None), P(AXES, None), P()),
        check_vma=False,
    )
```

```python
import functools

import jax
import jax.numpy as jnp
from jax import lax
from jax.experimental import pallas as pl
from jax.experimental.pallas import tpu as pltpu
from jax.sharding import PartitionSpec as P

F32 = jnp.float32
BF16 = jnp.bfloat16
SEND = jnp.float16
SIDE = 4
AXES = ("blk", "group")
LANES = 128
LOG2_E = 1.4426950408889634
TAIL = 16
CONTRACT_LAST = (((1,), (1,)), ((), ()))
CONTRACT_FIRST = (((0,), (0,)), ((), ()))


def place(x, y, z, core):
    return (y * 2 + x % 2) * 16 + (z * 2 + x // 2) * 2 + core


def pairs(move):
    found = []
    for x in range(SIDE):
        for y in range(SIDE):
            for z in range(SIDE):
                for core in range(2):
                    found.append((place(x, y, z, core), place(*move(x, y, z, core))))
    return found


def send(values, move):
    return lax.ppermute(values, AXES, pairs(move))


def pair_move(x, y, z, core):
    return (x ^ 1 if core == 0 else 3 - x, y, z, core)


def column_move(x, y, z, core):
    return (3 - x if core == 0 else x ^ 1, y, z, core)


def to_sibling(x, y, z, core):
    return (x, y, z, 1 - core)


def pair_step(step):
    return lambda x, y, z, core: (
        (x, y, (z + step) % SIDE, core) if core == 0 else (x, (y + step) % SIDE, z, core)
    )


def column_step(step):
    return lambda x, y, z, core: (
        (x, (y + step) % SIDE, z, core) if core == 0 else (x, y, (z + step) % SIDE, core)
    )


STEPS = (3, 2, 1)


def on_core():
    return lax.rem(lax.axis_index("group"), 2)


def row_norm_of(wide):
    return jnp.sqrt(jnp.sum(wide * wide, axis=1, keepdims=True) + 1e-06)


def column_of(weight_row, width):
    return jnp.transpose(jnp.broadcast_to(weight_row, (width, weight_row.shape[1])))


def prepare_kernel(img_ref, txt_ref, wgt_ref, pair_out, column_out):
    rows, width = img_ref.shape
    img = img_ref[...].astype(F32)
    img = (img / row_norm_of(img)).astype(BF16)
    txt = txt_ref[...].astype(F32)
    txt = (txt / row_norm_of(txt)).astype(BF16)
    here = pl.ds(0, rows)
    for out in (pair_out, column_out):
        out[pl.ds(rows, TAIL), :] = jnp.zeros((TAIL, width), BF16)
        out[pl.ds(rows, TAIL), pl.ds(0, rows)] = jnp.broadcast_to(wgt_ref[...], (TAIL, rows))

    @pl.when(on_core() == 0)
    def _():
        pair_out[here, :] = img
        column_out[here, :] = txt

    @pl.when(on_core() == 1)
    def _():
        pair_out[here, :] = txt
        column_out[here, :] = img


def join_kernel(log_scale_ref, bias_ref, *refs):
    pair_refs, column_refs, (pair_out, column_out, given) = refs[:2], refs[2:6], refs[6:]
    given[0:1, :] = jnp.exp(jnp.full((1, LANES), log_scale_ref[0], F32))
    given[1:2, :] = jnp.full((1, LANES), bias_ref[0], F32)
    for blocks, out in ((pair_refs, pair_out), (column_refs, column_out)):
        rows = blocks[0].shape[0] - TAIL
        tail = pl.ds(len(blocks) * rows, TAIL)
        out[tail, :] = jnp.zeros((TAIL, out.shape[1]), BF16)
        for index, block in enumerate(blocks):
            out[pl.ds(index * rows, rows), :] = block[pl.ds(0, rows), :]
            out[tail, pl.ds(index * rows, rows)] = block[pl.ds(rows, TAIL), pl.ds(0, rows)]


def weights_of(block, rows, first):
    return block[pl.ds(2 * rows, TAIL), :][0:1, first : first + rows].astype(F32)


def take_pairs(blocks, rows_out, wgt_out):
    rows = rows_out.shape[0] // (2 * SIDE)
    for step, block in enumerate(blocks):
        for chip in range(2):
            there = pl.ds((chip * SIDE + step) * rows, rows)
            rows_out[there, :] = block[pl.ds(chip * rows, rows), :]
            if wgt_out is not None:
                wgt_out[there, :] = column_of(weights_of(block, rows, chip * rows), LANES)


def take_columns(blocks, rows_out, wgt_out):
    span = rows_out.shape[0] // len(blocks)
    for index, block in enumerate(blocks):
        there = pl.ds(index * span, span)
        rows_out[there, :] = block[pl.ds(0, span), :]
        if wgt_out is not None:
            weight = block[pl.ds(span, TAIL), :][0:1, :span].astype(F32)
            wgt_out[there, :] = column_of(weight, LANES)


def score_part(img_all, wgt_all, txt_all, scale, bias, first, coef_out, weighted_out, grad_out, sums_out):
    count, width = img_all.shape
    scale_two, bias_two = scale * LOG2_E, bias * LOG2_E
    span = 256
    rows = 128
    zero = jnp.zeros((8, LANES), F32)
    loss, diff, score = zero, zero, zero
    same = lax.broadcasted_iota(jnp.int32, (rows, LANES), 0) == lax.broadcasted_iota(
        jnp.int32, (rows, LANES), 1
    )

    def fold(values):
        return jnp.sum(values.reshape(-1, 8, LANES), axis=0)

    def scores_of(part):
        img = img_all[pl.ds(span * part, span), :]
        return lax.dot_general(img, txt_all[...], CONTRACT_LAST, preferred_element_type=F32)

    def gradient_of(part):
        here = pl.ds(span * part, span)
        there = pl.ds(first + span * part, span)
        grad_out[here, :] = jnp.dot(coef_out[there, :], txt_all[...], preferred_element_type=F32)

    parts = count // span
    scores = scores_of(0)
    for part in range(parts):
        next_scores = scores_of(part + 1) if part + 1 < parts else None
        if part:
            gradient_of(part - 1)
        here = pl.ds(span * part, span)
        there = pl.ds(first + span * part, span)
        weight = wgt_all[here, :]
        weighted_out[there, :] = (
            img_all[here, :].astype(F32) * jnp.tile(weight, (1, width // LANES))
        ).astype(BF16)
        for tile in range(scores.shape[1] // LANES):
            score_tile = scores[:, tile * LANES : (tile + 1) * LANES]
            grown = jnp.exp2(score_tile * scale_two + bias_two)
            beyond = 1.0 + grown
            diffs = grown / beyond
            if first == 0 and part == 0 and tile == 0:
                diffs = jnp.concatenate(
                    [jnp.where(same, diffs[:rows] - 1.0, diffs[:rows]), diffs[rows:]], axis=0
                )
                matched = jnp.where(same, score_tile[:rows] * scale + bias, 0.0)
                loss = loss - fold(matched * weight[:rows])
            coef_out[there, pl.ds(tile * LANES, LANES)] = diffs.astype(BF16)
            if tile == 0:
                over, diff_row, score_row = grown, diffs, diffs * score_tile
            else:
                over = over * beyond + grown
                diff_row = diff_row + diffs
                score_row = score_row + diffs * score_tile
        loss = loss + fold(jnp.log1p(over) * weight)
        diff = diff + fold(diff_row * weight)
        score = score + fold(score_row * weight)
        scores = next_scores
    gradient_of(parts - 1)
    sums_out[0] = loss
    sums_out[1] = score
    sums_out[2] = diff


def own_kernel(given, *refs):
    pair_refs, column_refs = refs[:4], refs[4:6]
    grad_out, coef_out, weighted_out, sums_out, txt_all, img_all, wgt_all = refs[6:]

    @pl.when(on_core() == 0)
    def _():
        take_pairs(pair_refs, img_all, wgt_all)
        take_columns(column_refs, txt_all, None)

    @pl.when(on_core() == 1)
    def _():
        take_columns(column_refs, img_all, wgt_all)
        take_pairs(pair_refs, txt_all, None)

    score_part(
        img_all, wgt_all, txt_all, given[0:1, :], given[1:2, :], 0, coef_out, weighted_out, grad_out, sums_out
    )


def sibling_kernel(chip, given, *refs):
    pair_refs, column_ref, txt_all = refs[:4], refs[4], refs[5]
    grad_out, coef_out, weighted_out, sums_out, img_all, wgt_all = refs[8:]
    span = img_all.shape[0]
    rows = span // SIDE

    @pl.when(on_core() == 0)
    def _():
        take_columns((column_ref,), img_all, wgt_all)

    @pl.when(on_core() == 1)
    def _():
        for step, block in enumerate(pair_refs):
            there = pl.ds(step * rows, rows)
            img_all[there, :] = block[pl.ds(chip * rows, rows), :]
            wgt_all[there, :] = column_of(weights_of(block, rows, chip * rows), LANES)

    score_part(
        img_all, wgt_all, txt_all, given[0:1, :], given[1:2, :], (2 + chip) * span, coef_out, weighted_out, grad_out, sums_out
    )


def text_kernel(*refs):
    sums_refs, wgt_ref, coef, weighted = refs[:3], *refs[3:6]
    near_out, far_out, sums_out = refs[6:]
    span = near_out.shape[0]
    for chip, out in enumerate((near_out, far_out)):
        here = pl.ds(chip * span, span)
        out[...] = lax.dot_general(
            coef[:, here], weighted[...], CONTRACT_FIRST, preferred_element_type=F32
        )
    lane = lax.broadcasted_iota(jnp.int32, (1, LANES), 1)
    row = jnp.where(lane == 3, jnp.sum(wgt_ref[...].astype(F32), axis=1, keepdims=True), 0.0)
    for kind in range(3):
        part = jnp.sum(sum(ref[kind] for ref in sums_refs), axis=0, keepdims=True)
        row = row + jnp.where(lane == kind, jnp.sum(part, axis=1, keepdims=True), 0.0)
    sums_out[...] = jnp.broadcast_to(row, sums_out.shape)


def merge_kernel(own_grad, near_moved, far_moved, near_txt, far_txt, *outs):
    pair_keep, pair_send, column_keep, column_send = outs
    span = near_txt.shape[0]
    rows = span // SIDE

    def put_pair(chip, step, values):
        there = pl.ds(chip * rows, rows)
        if step == 0:
            pair_keep[there, :] = values
        else:
            pair_send[step - 1, there, :] = values

    for chip, (moved, txt, column) in enumerate(
        ((near_moved, near_txt, column_keep), (far_moved, far_txt, column_send))
    ):
        for step in range(SIDE):
            here = pl.ds(step * rows, rows)
            img_here = pl.ds(chip * span + step * rows, rows)

            @pl.when(on_core() == 0)
            def _():
                put_pair(chip, step, own_grad[img_here, :] + moved[here, :])
                column[here, :] = txt[here, :]

            @pl.when(on_core() == 1)
            def _():
                put_pair(chip, step, txt[here, :])
                column[here, :] = own_grad[img_here, :] + moved[here, :]


def back_kernel(given, img_ref, txt_ref, wgt_ref, pair_sum, column_sum, img_out, txt_out):
    rows, width = img_ref.shape
    pair_count = float(rows * 2 * SIDE**3)
    scale = jnp.tile(given[0:1, :], (1, width // LANES))
    first = on_core() == 0

    def back(gradient, values):
        norm = row_norm_of(values)
        unit = values / norm
        inner = jnp.sum(unit * gradient, axis=1, keepdims=True)
        return pair_count * (gradient - unit * inner) / norm

    weight = jnp.tile(column_of(wgt_ref[...].astype(F32), LANES), (1, width // LANES))
    img_sum = jnp.where(first, pair_sum[...], column_sum[...])
    txt_sum = jnp.where(first, column_sum[...], pair_sum[...])
    img_out[...] = back(scale * weight * img_sum, img_ref[...].astype(F32))
    txt_out[...] = back(scale * txt_sum, txt_ref[...].astype(F32))


def finish_kernel(given, sums_ref, img_back, txt_back, img_out, txt_out, scalar_out):
    lane = lax.broadcasted_iota(jnp.int32, (1, LANES), 1)
    sums = jnp.sum(sums_ref[...], axis=0, keepdims=True)
    total = jnp.sum(jnp.where(lane == 3, sums, 0.0), axis=1, keepdims=True)
    share = 1.0 / total
    img_out[...] = img_back[...] * share
    txt_out[...] = txt_back[...] * share
    ratio = jnp.where(lane == 1, given[0:1, :], 1.0) * sums / total
    for kind in range(3):
        scalar_out[kind] = jnp.sum(jnp.where(lane == kind, ratio, 0.0))


VMEM_MIB = 24
LONG_FLOPS = 4 * 10**10
IN_VMEM = pl.BlockSpec(memory_space=pltpu.VMEM)
IN_SMEM = pl.BlockSpec(memory_space=pltpu.SMEM)


def call(kernel, shapes, scalars, arrays, flops, moved, scratch=(), limit=16, aliases=None):
    return pl.pallas_call(
        kernel,
        out_shape=[jax.ShapeDtypeStruct(shape, kind) for shape, kind in shapes],
        in_specs=[IN_SMEM] * len(scalars) + [IN_VMEM] * len(arrays),
        out_specs=[IN_SMEM if len(shape) == 1 else IN_VMEM for shape, kind in shapes],
        scratch_shapes=list(scratch),
        input_output_aliases=aliases or {},
        compiler_params=pltpu.CompilerParams(vmem_limit_bytes=limit * 2**20),
        cost_estimate=pl.CostEstimate(flops=flops, bytes_accessed=moved, transcendentals=0),
    )(*scalars, *arrays)


def body(image_embeds, text_embeds, pair_weights, log_scale, bias):
    rows, width = image_embeds.shape
    span, tall = 2 * rows, 2 * SIDE * rows
    devices = 2 * SIDE**3
    weight_row = pair_weights.reshape(1, rows)
    pair_own, column_own = call(
        prepare_kernel,
        [((rows + TAIL, width), BF16)] * 2,
        [],
        [image_embeds, text_embeds, weight_row],
        2 * 8 * rows * width,
        8 * rows * width,
    )
    column_near = [column_own] + [send(column_own, column_step(step)) for step in STEPS]
    pair_near = [pair_own, send(pair_own, pair_move)]
    pair_all, column_all, given = call(
        join_kernel,
        [((span + TAIL, width), BF16), ((SIDE * rows + TAIL, width), BF16), ((8, LANES), F32)],
        [log_scale, bias],
        pair_near + column_near,
        1,
        24 * rows * width,
    )
    pairs_in = [pair_all] + [send(pair_all, pair_step(step)) for step in STEPS]
    columns_in = [column_all, send(column_all, column_move)]
    pairs_sib = [send(block, to_sibling) for block in pairs_in]
    columns_sib = [send(block, to_sibling) for block in columns_in]
    half = 4 * tall * tall * width
    flat = (tall, width)
    sums_shape = ((3, 8, LANES), F32)

    def images_kept(count):
        return [pltpu.VMEM((count, width), BF16), pltpu.VMEM((count, LANES), F32)]

    shared = [((2 * tall, tall), BF16), ((2 * tall, width), BF16)]
    own_grad, coef, weighted, own_sums, txt_all = call(
        own_kernel,
        [(flat, F32)] + shared + [sums_shape, (flat, BF16)],
        [],
        [given] + pairs_in + columns_in,
        half,
        16 * tall * width,
        images_kept(tall),
        VMEM_MIB,
    )
    moved, sums = [], [own_sums]
    for chip in range(2):
        count = tall // 2
        sib_grad, coef, weighted, sib_sums = call(
            functools.partial(sibling_kernel, chip),
            [((count, width), F32)] + shared + [sums_shape],
            [],
            [given] + pairs_sib + [columns_sib[chip], txt_all, coef, weighted],
            half // 2,
            8 * tall * width,
            images_kept(count),
            VMEM_MIB,
            {7: 1, 8: 2},
        )
        moved.append(send(sib_grad, to_sibling))
        sums.append(sib_sums)
    near_txt, far_txt, sums = call(
        text_kernel,
        [((SIDE * rows, width), F32)] * 2 + [((devices, LANES), F32)],
        [],
        sums + [weight_row, coef, weighted],
        half,
        12 * tall * width,
        (),
        VMEM_MIB,
    )
    pair_keep, pair_send, column_keep, column_send = call(
        merge_kernel,
        [
            ((span, width), F32),
            ((SIDE - 1, span, width), F32),
            ((SIDE * rows, width), F32),
            ((SIDE * rows, width), F32),
        ],
        [],
        [own_grad] + moved + [near_txt, far_txt],
        1,
        24 * tall * width,
    )
    column_sum = column_keep + send(column_send.astype(SEND), column_move).astype(F32)
    pair_sum = pair_keep + 0.0 * column_sum[:span]
    for index, step in enumerate(STEPS):
        pair_sum = pair_sum + send(pair_send[index].astype(SEND), pair_step(-step)).astype(F32)
    all_sums = lax.all_to_all(sums, AXES, 0, 0, tiled=True)
    pair_last = pair_sum[:rows] + send(pair_sum[rows:].astype(SEND), pair_move).astype(F32)
    column_last = column_sum[:rows]
    for index, step in enumerate(STEPS):
        block = column_sum[(index + 1) * rows : (index + 2) * rows]
        column_last = column_last + send(block.astype(SEND), column_step(-step)).astype(F32)
    img_back, txt_back = call(
        back_kernel,
        [((rows, width), F32)] * 2,
        [],
        [given, image_embeds, text_embeds, weight_row, pair_last, column_last],
        LONG_FLOPS,
        24 * rows * width,
    )
    grad_image, grad_text, scalars = call(
        finish_kernel,
        [((rows, width), F32), ((rows, width), F32), ((3,), F32)],
        [],
        [given, all_sums, img_back, txt_back],
        2 * rows * width,
        16 * rows * width,
    )
    return grad_image, grad_text, scalars


def solution(mesh):
    placed = (P(AXES, None), P(AXES, None), P(AXES), P(), P())
    return jax.shard_map(
        body,
        mesh=mesh,
        in_specs=placed,
        out_specs=(P(AXES, None), P(AXES, None), P()),
        check_vma=False,
    )
```
